128 devices in a mesh: grp: 8 (over y, core), morton: 16 (over z, x).
Axes of the slice: x: 4, y: 4, z: 4, core: 2. Of those that a mesh axis runs over, the one named last changes fastest.
Arguments:
- density: bfloat16 [65536, 512], P(('morton', 'grp')), may hold values from -6 to 6
- send_list: int32 [128, 2048], P(('morton', 'grp')), may hold values from 0 to 511
- v_src: int32 [65536, 32], P(('morton', 'grp')), may hold values from 0 to 2560
- v_type: int32 [65536, 32], P(('morton', 'grp')), may hold values from 0 to 11
- coarse_src: int32 [8192, 32], P(('morton', 'grp')), may hold values from 0 to 512
- coarse_type: int32 [8192, 32], P(('morton', 'grp')), may hold values from 0 to 11
- m2l_ops: bfloat16 [12, 512, 512], replicated, may hold values from -0.046875 to 0.046875
- coarse_ops: bfloat16 [12, 512, 512], replicated, may hold values from -0.046875 to 0.046875
- m2m_ops: bfloat16 [8, 512, 512], replicated, may hold values from -0.09375 to 0.09375
- l2l_ops: bfloat16 [8, 512, 512], replicated, may hold values from -0.25 to 0.25
Outputs:
- local_field: float32 [65536, 512], P(('morton', 'grp'))
The draws below stay inside these ranges and needn't reach their ends.
Inputs may be any that keep to these rules, and one draw needn't show every extreme that they name: `send_list`: entries are local box indices of the sending device. `v_src`: the value 2560 names the zero row (an empty slot). `coarse_src`: the value 512 names the zero row (an empty slot).
All inputs are finite; a program needn't handle non-finite values.
Results may differ from the reference program's by a relative error of at most 0.004.
Values may be sent and summed in bfloat16 or wider, within the bound.
A program may use at most 128 MiB of HBM per device.

```python
import jax
import jax.numpy as jnp
from jax import lax

P_SIZE = 256
BOX_DEV = 512
GHOST = 16
VMAX = 32
CVMAX = 32
TYPES = 12
BOXES = 65536
PARENTS = 8192
ROWS = 2560
GROUP_ROWS = 512
N_GRP = 8
N_MORTON = 16
DEVICES = 128


def set_ends(entries, stream_key, smallest, largest):
    longest = entries.shape.index(max(entries.shape))
    spots = []
    for shift in (0, 1):
        where = [jax.random.randint(jax.random.fold_in(stream_key, axis), (), 0, length) for axis, length in enumerate(entries.shape)]
        where[longest] = (where[longest] + shift) % entries.shape[longest]
        spots.append(tuple(where))
    return entries.at[spots[0]].set(smallest).at[spots[1]].set(largest)


def steps_of(rng, shape, shards, low, largest):
    def one(axis_at, parts):
        steps = jax.random.uniform(jax.random.fold_in(jax.random.fold_in(rng, 6), axis_at), (parts,), jnp.float32, low / len(shards), largest / len(shards))
        return jnp.repeat(jnp.exp(steps), shape[axis_at] // parts).reshape((-1,) + (1,) * (len(shape) - axis_at - 1))

    factor_of = one(*shards[0])
    for cut in shards[1:]:
        factor_of = factor_of * one(*cut)
    return factor_of


def centred(own_key, dims, width, limit, split=(), kind=jnp.bfloat16):
    values = jax.random.normal(own_key, dims, jnp.float32) * width
    if len(split) > 0:
        values = steps_of(own_key, dims, split, -0.22, 0.18) * values
    return jnp.clip(values, min=-limit, max=limit).astype(kind)


def setup_inputs(seed: int = 0) -> dict:
    keys = jax.random.split(jax.random.key(seed), 11)
    return {
        "density": centred(keys[0], (BOXES, 2 * P_SIZE), 1.0, 6.0, ((0, 128),)),
        "send_list": set_ends(jax.random.randint(keys[1], (DEVICES, DEVICES * GHOST), 0, BOX_DEV), jax.random.fold_in(keys[1], 1), 0, BOX_DEV - 1).astype(jnp.int32),
        "v_src": set_ends(jax.random.randint(keys[2], (BOXES, VMAX), 0, ROWS + 1), jax.random.fold_in(keys[2], 1), 0, ROWS).astype(jnp.int32),
        "v_type": set_ends(jax.random.randint(keys[3], (BOXES, VMAX), 0, TYPES), jax.random.fold_in(keys[3], 1), 0, TYPES - 1).astype(jnp.int32),
        "coarse_src": set_ends(jax.random.randint(keys[4], (PARENTS, CVMAX), 0, GROUP_ROWS + 1), jax.random.fold_in(keys[4], 1), 0, GROUP_ROWS).astype(jnp.int32),
        "coarse_type": set_ends(jax.random.randint(keys[5], (PARENTS, CVMAX), 0, TYPES), jax.random.fold_in(keys[5], 1), 0, TYPES - 1).astype(jnp.int32),
        "m2l_ops": centred(keys[6], (TYPES, 2 * P_SIZE, 2 * P_SIZE), (2 * P_SIZE * VMAX) ** -0.5, 0.046875),
        "coarse_ops": centred(keys[7], (TYPES, 2 * P_SIZE, 2 * P_SIZE), (2 * P_SIZE * CVMAX) ** -0.5, 0.046875),
        "m2m_ops": centred(keys[8], (8, 2 * P_SIZE, 2 * P_SIZE), (2 * P_SIZE * 8) ** -0.5, 0.09375),
        "l2l_ops": centred(keys[9], (8, 2 * P_SIZE, 2 * P_SIZE), (2 * P_SIZE) ** -0.5, 0.25),
    }


def apply_types(source_rows, sources, kinds, operators):
    picked = source_rows[sources].astype(jnp.float32)
    onehot = (kinds[:, :, None] == jnp.arange(TYPES, dtype=jnp.int32)[None, None, :]).astype(jnp.float32)
    typed = jnp.einsum('njt,njw->tnw', onehot, picked).astype(jnp.bfloat16)
    return jnp.einsum('tnw,twv->nv', typed.astype(jnp.float32), operators.astype(jnp.float32))


def reference(density, send_list, v_src, v_type, coarse_src, coarse_type, m2l_ops, coarse_ops, m2m_ops, l2l_ops):
    devices = N_GRP * N_MORTON
    columns = 2 * P_SIZE
    multipoles = density.reshape(devices, BOX_DEV, columns)
    parents = jnp.einsum('dpkw,kwv->dpv', multipoles.reshape(devices, BOX_DEV // 8, 8, columns).astype(jnp.float32), m2m_ops.astype(jnp.float32)).astype(jnp.bfloat16)
    groups = parents.reshape(N_MORTON, N_GRP * (BOX_DEV // 8), columns)
    slot_index = send_list.reshape(devices, devices, GHOST)
    leaf_src = v_src.reshape(devices, BOX_DEV, VMAX)
    leaf_type = v_type.reshape(devices, BOX_DEV, VMAX)
    group_src = coarse_src.reshape(devices, BOX_DEV // 8, CVMAX)
    group_type = coarse_type.reshape(devices, BOX_DEV // 8, CVMAX)
    empty_row = jnp.zeros((1, columns), jnp.bfloat16)
    ranks = jnp.arange(devices, dtype=jnp.int32)
    rank_device = (ranks % N_MORTON) * N_GRP + ranks // N_MORTON

    def per_device(device):
        morton_index = device // N_GRP
        grp_index = device % N_GRP
        my_rank = grp_index * N_MORTON + morton_index
        senders = rank_device[:, None]
        ghosts = multipoles[senders, slot_index[rank_device, my_rank, :]].reshape(devices * GHOST, columns)
        source_rows = jnp.concatenate([multipoles[device], ghosts, empty_row], axis=0)
        far_field = apply_types(source_rows, leaf_src[device], leaf_type[device], m2l_ops)
        group_rows = jnp.concatenate([groups[morton_index], empty_row], axis=0)
        coarse = apply_types(group_rows, group_src[device], group_type[device], coarse_ops).astype(jnp.bfloat16)
        from_parent = jnp.einsum('pw,kwv->pkv', coarse.astype(jnp.float32), l2l_ops.astype(jnp.float32)).reshape(BOX_DEV, columns)
        return far_field + from_parent

    result = lax.map(per_device, jnp.arange(devices, dtype=jnp.int32))
    return result.reshape(devices * BOX_DEV, columns)
```

```python
import functools

import jax
import jax.numpy as jnp
from jax import lax
from jax.experimental import pallas as pl
from jax.experimental.pallas import tpu as pltpu
from jax.sharding import PartitionSpec as P

MESH = pl.DeviceIdType.MESH
BF16 = jnp.bfloat16
F32 = jnp.float32
I32 = jnp.int32

DEVICES = 128
GHOST = 16
BOXES = 512
WIDTH = 512
TYPES = 12
SLOTS = 32
PARENTS = 64
PART = 512
LO = 256
KEYS = 2 * TYPES * 8
NONE = 255.0


def dot(a, b):
    return jnp.dot(a, b, preferred_element_type=F32)


def dot_t(a, b):
    return lax.dot_general(a, b, (((1,), (1,)), ((), ())), preferred_element_type=F32)


def iota(shape, dim):
    return lax.broadcasted_iota(I32, shape, dim)


def to_lanes(values):
    n = values.shape[0]
    spread = (iota((SLOTS, 8 * SLOTS), 1) % SLOTS == iota((SLOTS, 8 * SLOTS), 0)).astype(F32).astype(BF16)
    wide = dot(values.astype(F32).astype(BF16), spread)
    own = iota((n, 8 * SLOTS), 0) % 8 == iota((n, 8 * SLOTS), 1) // SLOTS
    wide = jnp.where(own, wide, 0.0).astype(BF16)
    rows = (iota((n // 8, n), 1) // 8 == iota((n // 8, n), 0)).astype(F32).astype(BF16)
    return dot(rows, wide)


def write_keys(column, kind, parts, key_ref, lo_ref):
    n = column.shape[0]
    hi = column // LO
    key = (hi % 2) * (TYPES * 8) + kind * 8 + iota((n, SLOTS), 0) % 8
    key_row = to_lanes(key)
    part_row = to_lanes(hi // 2)
    lo_ref[...] = to_lanes(column % LO)
    for part in range(parts):
        key_ref[part] = jnp.where(part_row == float(part), key_row, NONE)


def one_hot(row, count):
    wide = jnp.broadcast_to(row, (16, row.shape[1])).astype(BF16)
    shape = (count // 16, 16, row.shape[1])
    index = (iota(shape, 0) * 16 + iota(shape, 1)).astype(F32).astype(BF16)
    return jnp.where(wide[None] == index, jnp.ones((), BF16), jnp.zeros((), BF16)).reshape(count, row.shape[1])


def build_counts(pair, parts, slots, key_ref, lo_ref, count_ref):
    results = []
    for u in range(2):
        group = 2 * pair + u
        low = one_hot(lo_ref[pl.ds(group, 1), :], LO)
        hot = jnp.concatenate([one_hot(key_ref[part, pl.ds(group, 1), :], KEYS) for part in parts], axis=0)
        results.append(dot_t(hot, low))
    row = pl.multiple_of(pair * 16, 16)
    for j, slot in enumerate(slots):
        for half in range(2):
            first = j * KEYS + half * (KEYS // 2)
            both = [r[first : first + KEYS // 2].reshape(TYPES, 8, LO) for r in results]
            count_ref[slot, :, pl.ds(row, 16), half * LO : (half + 1) * LO] = jnp.concatenate(both, axis=1).astype(BF16)


def step_of(i):
    s = i // 32
    dy = (i // 8) % 4
    dz = (i // 2) % 4
    dc = i % 2
    dx = (s + 8 - dy - dz) % 4
    return dy, dc, dz, dx


def kernel(
    density_h, send_h, v_src_h, v_type_h, c_src_h, c_type_h, m2l_h, cops_h, m2m_h, l2l_h,
    out_ref,
    dens, send, v_src, v_type, c_src, c_type, m2l, cops, octant,
    outgoing, ghosts, parents, table, counts, typed, from_parent,
    key_ref, lo_ref, ckey_ref, clo_ref, ccounts,
    load_sem, weight_sem, send_sem, recv_sem, psend_sem, precv_sem,
):
    g = lax.axis_index("grp")
    m = lax.axis_index("morton")
    me = g * 16 + m
    my, mc, mz, mx = g // 2, g % 2, m // 4, m % 4

    loads = []
    for j, (src, dst) in enumerate(
        ((density_h, dens), (send_h, send), (v_src_h, v_src), (v_type_h, v_type), (c_src_h, c_src), (c_type_h, c_type))
    ):
        loads.append(pltpu.make_async_copy(src, dst, load_sem.at[j]))
    load_m2m = pltpu.make_async_copy(m2m_h, octant, weight_sem.at[0])
    load_cops = pltpu.make_async_copy(cops_h, cops, weight_sem.at[1])
    load_m2l = pltpu.make_async_copy(m2l_h, m2l, weight_sem.at[2])
    load_l2l = pltpu.make_async_copy(l2l_h, octant, weight_sem.at[3])
    for load in loads[:2]:
        load.start()
    load_m2m.start()
    for load in loads[2:]:
        load.start()

    barrier = pltpu.get_barrier_semaphore()

    def greet(i, carry):
        other = (me + i) % DEVICES
        pl.semaphore_signal(barrier, inc=1, device_id=(other // 16, other % 16), device_id_type=MESH)
        return carry

    lax.fori_loop(1, DEVICES, greet, 0)

    loads[0].wait()
    loads[1].wait()
    wanted = jnp.concatenate([send[:, q * 128 : (q + 1) * 128] for q in range(16)], axis=0).astype(F32)
    wanted = jnp.concatenate([wanted, jnp.zeros((112, 128), F32)], axis=0).T
    for q in range(16):
        column = jnp.broadcast_to(wanted[:, q : q + 1], (128, BOXES))
        hot = jnp.where(column == iota((128, BOXES), 1).astype(F32), 1.0, 0.0).astype(BF16)
        outgoing[q * 128 : (q + 1) * 128, :] = dot(hot, dens[...]).astype(BF16)

    r = iota((BOXES, BOXES), 0)
    order = (iota((BOXES, BOXES), 1) == (r % PARENTS) * 8 + r // PARENTS).astype(F32).astype(BF16)
    by_octant = dot(order, dens[...]).astype(BF16)
    load_m2m.wait()
    total = dot(by_octant[0:PARENTS], octant[0])
    for k in range(1, 8):
        total = total + dot(by_octant[k * PARENTS : (k + 1) * PARENTS], octant[k])
    mine = total.astype(BF16)
    parents[...] = mine
    my_rows = pl.ds(pl.multiple_of(g * PARENTS, PARENTS), PARENTS)
    table[my_rows, :] = mine
    ghosts[0:GHOST, :] = outgoing[pl.ds(pl.multiple_of(me * GHOST, GHOST), GHOST), :]

    load_l2l.start()
    load_cops.start()
    load_m2l.start()

    pl.semaphore_wait(barrier, DEVICES - 1)

    for i in range(1, 8):
        pltpu.make_async_remote_copy(
            src_ref=parents, dst_ref=table.at[my_rows], send_sem=psend_sem, recv_sem=precv_sem,
            device_id=((g + i) % 8, m), device_id_type=MESH,
        ).start()

    def send_rows(i):
        dy, dc, dz, dx = step_of(i)
        g2 = ((my + dy) % 4) * 2 + (mc + dc) % 2
        m2 = ((mz + dz) % 4) * 4 + (mx + dx) % 4
        there = pl.multiple_of((g2 * 16 + m2) * GHOST, GHOST)
        pltpu.make_async_remote_copy(
            src_ref=outgoing.at[pl.ds(there, GHOST)],
            dst_ref=ghosts.at[pl.ds(pl.multiple_of(i * GHOST, GHOST), GHOST)],
            send_sem=send_sem, recv_sem=recv_sem.at[i // 32],
            device_id=(g2, m2), device_id_type=MESH,
        ).start()

    def send_first(i, carry):
        send_rows(i)
        return carry

    lax.fori_loop(1, 32, send_first, 0)

    for load in loads[2:]:
        load.wait()
    source = v_src[...]
    sender = (source - BOXES) // GHOST
    dx = (mx + 4 - sender % 4) % 4
    dz = (mz + 4 - (sender // 4) % 4) % 4
    dc = (mc + 2 - (sender // 16) % 2) % 2
    dy = (my + 4 - (sender // 32) % 4) % 4
    place = ((dx + dy + dz) % 4) * 32 + dy * 8 + dz * 2 + dc
    moved = BOXES + place * GHOST + source % GHOST
    column = jnp.where(source < BOXES, source, jnp.where(source < BOXES + DEVICES * GHOST, moved, 5 * PART))
    write_keys(column, v_type[...], 5, key_ref, lo_ref)
    write_keys(c_src[...], c_type[...], 1, ckey_ref, clo_ref)

    def build_first(pair, carry):
        for j in range(3):
            send_rows(32 + 3 * pair + j)
        build_counts(pair, (0, 1, 2), (0, 1, 2), key_ref, lo_ref, counts)
        return carry

    lax.fori_loop(0, 32, build_first, 0)

    def own(t, carry):
        typed[t] = dot(counts[0, t], dens[...])
        return carry

    lax.fori_loop(0, TYPES, own, 0)

    def build_coarse(pair, carry):
        build_counts(pair, (0,), (0,), ckey_ref, clo_ref, ccounts)
        return carry

    lax.fori_loop(0, 4, build_coarse, 0)
    rest = table.at[pl.ds(0, 7 * PARENTS)]
    pltpu.make_async_remote_copy(
        src_ref=rest, dst_ref=rest, send_sem=psend_sem, recv_sem=precv_sem, device_id=((g + 1) % 8, m), device_id_type=MESH
    ).wait_recv()
    load_cops.wait()

    def coarse_step(t, total):
        kinds = dot(ccounts[0, t], table[...]).astype(BF16)
        return total + dot(kinds, cops[t])

    coarse = lax.fori_loop(0, TYPES, coarse_step, jnp.zeros((PARENTS, WIDTH), F32)).astype(BF16)
    load_l2l.wait()
    for k in range(8):
        from_parent[:, k, :] = dot(coarse, octant[k])
    out_ref[...] = from_parent[...].reshape(BOXES, WIDTH)

    def arrived(part):
        first = GHOST if part == 0 else 0
        rows = ghosts.at[pl.ds(part * PART + first, PART - first)]
        pltpu.make_async_remote_copy(
            src_ref=rows, dst_ref=rows, send_sem=send_sem, recv_sem=recv_sem.at[part],
            device_id=((g + 1) % 8, m), device_id_type=MESH,
        ).wait_recv()

    def add_part(slot, part):
        def body(t, carry):
            typed[t] += dot(counts[slot, t], ghosts[part * PART : (part + 1) * PART, :])
            return carry

        lax.fori_loop(0, TYPES, body, 0)

    arrived(0)
    add_part(1, 0)

    def build_second(pair, carry):
        build_counts(pair, (3, 4), (0, 1), key_ref, lo_ref, counts)
        return carry

    lax.fori_loop(0, 32, build_second, 0)
    arrived(1)
    add_part(2, 1)
    arrived(2)
    add_part(0, 2)
    load_m2l.wait()
    arrived(3)

    def finish(t, carry):
        kinds = typed[t] + dot(counts[1, t], ghosts[3 * PART : 4 * PART, :])
        out_ref[...] += dot(kinds.astype(BF16), m2l[t])
        return carry

    lax.fori_loop(0, TYPES, finish, 0)

    sent = outgoing.at[pl.ds(0, (DEVICES - 1) * GHOST)]
    pltpu.make_async_remote_copy(
        src_ref=sent, dst_ref=sent, send_sem=send_sem, recv_sem=recv_sem.at[0],
        device_id=((g + 1) % 8, m), device_id_type=MESH,
    ).wait_send()
    pltpu.make_async_remote_copy(
        src_ref=rest, dst_ref=rest, send_sem=psend_sem, recv_sem=precv_sem, device_id=((g + 1) % 8, m), device_id_type=MESH
    ).wait_send()


def shards(density, send_list, v_src, v_type, coarse_src, coarse_type, m2l_ops, coarse_ops, m2m_ops, l2l_ops):
    dma = pltpu.SemaphoreType.DMA
    return pl.pallas_call(
        kernel,
        out_shape=jax.ShapeDtypeStruct((BOXES, WIDTH), F32),
        in_specs=[pl.BlockSpec(memory_space=pl.ANY)] * 10,
        out_specs=pl.BlockSpec(memory_space=pltpu.VMEM),
        scratch_shapes=[
            pltpu.VMEM((BOXES, WIDTH), BF16),
            pltpu.VMEM((1, DEVICES * GHOST), I32),
            pltpu.VMEM((BOXES, SLOTS), I32),
            pltpu.VMEM((BOXES, SLOTS), I32),
            pltpu.VMEM((PARENTS, SLOTS), I32),
            pltpu.VMEM((PARENTS, SLOTS), I32),
            pltpu.VMEM((TYPES, WIDTH, WIDTH), BF16),
            pltpu.VMEM((TYPES, WIDTH, WIDTH), BF16),
            pltpu.VMEM((8, WIDTH, WIDTH), BF16),
            pltpu.VMEM((DEVICES * GHOST, WIDTH), BF16),
            pltpu.VMEM((DEVICES * GHOST, WIDTH), BF16),
            pltpu.VMEM((PARENTS, WIDTH), BF16),
            pltpu.VMEM((8 * PARENTS, WIDTH), BF16),
            pltpu.VMEM((3, TYPES, BOXES, PART), BF16),
            pltpu.VMEM((TYPES, BOXES, WIDTH), F32),
            pltpu.VMEM((PARENTS, 8, WIDTH), F32),
            pltpu.VMEM((5, BOXES // 8, 8 * SLOTS), F32),
            pltpu.VMEM((BOXES // 8, 8 * SLOTS), F32),
            pltpu.VMEM((1, PARENTS // 8, 8 * SLOTS), F32),
            pltpu.VMEM((PARENTS // 8, 8 * SLOTS), F32),
            pltpu.VMEM((1, TYPES, PARENTS, PART), BF16),
            dma((6,)),
            dma((4,)),
            dma,
            dma((4,)),
            dma,
            dma,
        ],
        compiler_params=pltpu.CompilerParams(
            collective_id=0, has_side_effects=True, vmem_limit_bytes=60 * 1024 * 1024
        ),
        cost_estimate=pl.CostEstimate(flops=25_000_000_000, bytes_accessed=30_000_000, transcendentals=0),
        name="far_field",
    )(density, send_list, v_src, v_type, coarse_src, coarse_type, m2l_ops, coarse_ops, m2m_ops, l2l_ops)


def solution(mesh):
    row = P(("morton", "grp"), None)
    return jax.shard_map(
        shards,
        mesh=mesh,
        in_specs=(row, row, row, row, row, row, P(), P(), P(), P()),
        out_specs=row,
        check_vma=False,
    )
```

```python
import jax
import jax.numpy as jnp
from jax import lax
from jax.experimental import pallas as pl
from jax.experimental.pallas import tpu as pltpu
from jax.sharding import PartitionSpec as P

MESH = pl.DeviceIdType.MESH
BF16 = jnp.bfloat16
F32 = jnp.float32
I32 = jnp.int32

DEVICES = 128
GHOST = 16
BOXES = 512
WIDTH = 512
TYPES = 12
SLOTS = 32
PARENTS = 64
LO = 256
KEYS = 2 * TYPES * 8
NONE = 255.0
ROWS = BOXES + DEVICES * GHOST
CHUNKS = WIDTH // 128


def dot(a, b):
    return jnp.dot(a, b, preferred_element_type=F32)


def dot_t(a, b):
    return lax.dot_general(a, b, (((1,), (1,)), ((), ())), preferred_element_type=F32)


def iota(shape, dim):
    return lax.broadcasted_iota(I32, shape, dim)


def to_lanes(values):
    n = values.shape[0]
    spread = (iota((SLOTS, 8 * SLOTS), 1) % SLOTS == iota((SLOTS, 8 * SLOTS), 0)).astype(F32).astype(BF16)
    wide = dot(values.astype(F32).astype(BF16), spread)
    own = iota((n, 8 * SLOTS), 0) % 8 == iota((n, 8 * SLOTS), 1) // SLOTS
    wide = jnp.where(own, wide, 0.0).astype(BF16)
    rows = (iota((n // 8, n), 1) // 8 == iota((n // 8, n), 0)).astype(F32).astype(BF16)
    return dot(rows, wide)


def write_keys(column, kind, key_ref, lo_ref):
    n = column.shape[0]
    hi = column // LO
    key = (hi % 2) * (TYPES * 8) + kind * 8 + iota((n, SLOTS), 0) % 8
    key_ref[...] = jnp.where(to_lanes(hi // 2) == 0.0, to_lanes(key), NONE)
    lo_ref[...] = to_lanes(column % LO)


def one_hot(row, count):
    wide = jnp.broadcast_to(row, (16, row.shape[1])).astype(BF16)
    shape = (count // 16, 16, row.shape[1])
    index = (iota(shape, 0) * 16 + iota(shape, 1)).astype(F32).astype(BF16)
    return jnp.where(wide[None] == index, jnp.ones((), BF16), jnp.zeros((), BF16)).reshape(count, row.shape[1])


def build_counts(pair, key_ref, lo_ref, count_ref):
    results = []
    for u in range(2):
        group = 2 * pair + u
        low = one_hot(lo_ref[pl.ds(group, 1), :], LO)
        results.append(dot_t(one_hot(key_ref[pl.ds(group, 1), :], KEYS), low))
    row = pl.multiple_of(pair * 16, 16)
    for half in range(2):
        first = half * (KEYS // 2)
        both = [r[first : first + KEYS // 2].reshape(TYPES, 8, LO) for r in results]
        count_ref[:, pl.ds(row, 16), half * LO : (half + 1) * LO] = jnp.concatenate(both, axis=1).astype(BF16)


def to_table(rows_ref, first, count, tab, at):
    for j in range(CHUNKS):
        part = rows_ref[first : first + count, j * 128 : (j + 1) * 128].astype(F32)
        tab[pl.ds(at * CHUNKS + j, count, stride=CHUNKS), :] = part


def pick(tab, start, picked, slot):
    place = (slot // 8) * (8 * CHUNKS) + slot % 8
    picked[pl.ds(place, CHUNKS, stride=8), :] = tab[pl.ds(start, CHUNKS), :]


def picked_rows(picked, count):
    tiles = picked[...].reshape(count // 8, CHUNKS, 8, 128)
    return [tiles[:, j].reshape(count, 128).astype(BF16) for j in range(CHUNKS)]


def step_of(i):
    s = i // 32
    dy = (i // 8) % 4
    dz = (i // 2) % 4
    dc = i % 2
    dx = (s + 8 - dy - dz) % 4
    return dy, dc, dz, dx


def kernel(
    density_h, send_h, v_src_h, v_type_h, c_src_h, c_type_h, m2l_h, cops_h, m2m_h, l2l_h,
    out_ref,
    dens, send, v_src, v_type, c_src, c_type, m2l, cops, octant,
    outgoing, ghosts, parents, group, typed, from_parent, tab, pick_0, pick_1, pick_2, pick_3, start_a, start_b, scaled,
    type_key, ckey_ref, clo_ref, ccounts,
    load_sem, weight_sem, index_sem, send_sem, recv_sem, psend_sem, precv_sem,
):
    g = lax.axis_index("grp")
    m = lax.axis_index("morton")
    me = g * 16 + m
    picks = (pick_0, pick_1, pick_2, pick_3)
    my, mc, mz, mx = g // 2, g % 2, m // 4, m % 4

    loads = []
    for j, (src, dst) in enumerate(
        ((density_h, dens), (send_h, send), (v_src_h, v_src), (v_type_h, v_type), (c_src_h, c_src), (c_type_h, c_type))
    ):
        loads.append(pltpu.make_async_copy(src, dst, load_sem.at[j]))
    load_m2m = pltpu.make_async_copy(m2m_h, octant, weight_sem.at[0])
    load_cops = pltpu.make_async_copy(cops_h, cops, weight_sem.at[1])
    load_m2l = pltpu.make_async_copy(m2l_h, m2l, weight_sem.at[2])
    load_l2l = pltpu.make_async_copy(l2l_h, octant, weight_sem.at[3])
    for load in loads[:2]:
        load.start()
    load_m2m.start()
    for load in loads[2:]:
        load.start()

    barrier = pltpu.get_barrier_semaphore()

    def greet(i, carry):
        other = (me + i) % DEVICES
        pl.semaphore_signal(barrier, inc=1, device_id=(other // 16, other % 16), device_id_type=MESH)
        return carry

    lax.fori_loop(1, DEVICES, greet, 0)

    loads[0].wait()
    to_table(dens, 0, BOXES, tab, 0)
    tab[ROWS * CHUNKS : (ROWS + 2) * CHUNKS, :] = jnp.zeros((2 * CHUNKS, 128), F32)
    loads[1].wait()

    for q in range(8):
        picked = picks[q % 4]
        for s in range(256):
            pick(tab, send[0, q * 256 + s] * CHUNKS, picked, s)
        for j, part in enumerate(picked_rows(picked, 256)):
            outgoing[q * 256 : (q + 1) * 256, j * 128 : (j + 1) * 128] = part

    ghosts[pl.ds(pl.multiple_of(me * GHOST, GHOST), GHOST), :] = outgoing[pl.ds(pl.multiple_of(me * GHOST, GHOST), GHOST), :]

    pl.semaphore_wait(barrier, DEVICES - 1)

    def send_rows(i, carry):
        dy, dc, dz, dx = step_of(i)
        g2 = ((my + dy) % 4) * 2 + (mc + dc) % 2
        m2 = ((mz + dz) % 4) * 4 + (mx + dx) % 4
        there = pl.multiple_of((g2 * 16 + m2) * GHOST, GHOST)
        pltpu.make_async_remote_copy(
            src_ref=outgoing.at[pl.ds(there, GHOST)],
            dst_ref=ghosts.at[pl.ds(pl.multiple_of(me * GHOST, GHOST), GHOST)],
            send_sem=send_sem, recv_sem=recv_sem,
            device_id=(g2, m2), device_id_type=MESH,
        ).start()
        return carry

    lax.fori_loop(1, 64, send_rows, 0)

    r = iota((BOXES, BOXES), 0)
    order = (iota((BOXES, BOXES), 1) == (r % PARENTS) * 8 + r // PARENTS).astype(F32).astype(BF16)
    by_octant = dot(order, dens[...]).astype(BF16)
    load_m2m.wait()
    total = dot(by_octant[0:PARENTS], octant[0])
    for k in range(1, 8):
        total = total + dot(by_octant[k * PARENTS : (k + 1) * PARENTS], octant[k])
    mine = total.astype(BF16)
    parents[...] = mine
    my_rows = pl.ds(pl.multiple_of(g * PARENTS, PARENTS), PARENTS)
    group[my_rows, :] = mine
    for i in range(1, 8):
        pltpu.make_async_remote_copy(
            src_ref=parents, dst_ref=group.at[my_rows], send_sem=psend_sem, recv_sem=precv_sem,
            device_id=((g + i) % 8, m), device_id_type=MESH,
        ).start()
    load_l2l.start()
    load_cops.start()
    load_m2l.start()
    lax.fori_loop(64, DEVICES, send_rows, 0)

    for load in loads[2:]:
        load.wait()
    scaled[...] = v_src[...] * CHUNKS
    kinds = v_type[...].T
    type_key[...] = to_lanes(kinds * 8 + iota((BOXES, SLOTS), 0) % 8)
    write_keys(c_src[...].T, c_type[...].T, ckey_ref, clo_ref)

    def build_coarse(pair, carry):
        build_counts(pair, ckey_ref, clo_ref, ccounts)
        return carry

    lax.fori_loop(0, 4, build_coarse, 0)
    rest = group.at[pl.ds(0, 7 * PARENTS)]
    pltpu.make_async_remote_copy(
        src_ref=rest, dst_ref=rest, send_sem=psend_sem, recv_sem=precv_sem, device_id=((g + 1) % 8, m), device_id_type=MESH
    ).wait_recv()
    load_cops.wait()

    def coarse_step(t, total):
        summed = dot(ccounts[t], group[...]).astype(BF16)
        return total + dot(summed, cops[t])

    coarse = lax.fori_loop(0, TYPES, coarse_step, jnp.zeros((PARENTS, WIDTH), F32)).astype(BF16)
    load_l2l.wait()
    for k in range(8):
        from_parent[:, k, :] = dot(coarse, octant[k])
    out_ref[...] = from_parent[...].reshape(BOXES, WIDTH)

    def fetch(block, stage):
        first = pl.multiple_of(jnp.minimum(block, 3) * 128, 128)
        return pltpu.make_async_copy(scaled.at[:, pl.ds(first, 128)], (start_a, start_b)[stage], index_sem.at[stage])

    fetch(0, 0).start()
    fetch(1, 1).start()
    load_m2l.wait()
    came = ghosts.at[pl.ds(0, (DEVICES - 1) * GHOST)]
    pltpu.make_async_remote_copy(
        src_ref=came, dst_ref=came, send_sem=send_sem, recv_sem=recv_sem,
        device_id=((g + 1) % 8, m), device_id_type=MESH,
    ).wait()
    to_table(ghosts, 0, DEVICES * GHOST, tab, BOXES)

    def pick_pair(stage, part):
        for u in range(2):
            for s in range(256):
                column = part * 16 + u * 8 + s // SLOTS
                pick(tab, (start_a, start_b)[stage][s % SLOTS, column], picks[2 * (part % 2) + u], s)

    def sum_pair(block, part):
        both = []
        for u in range(2):
            hot = one_hot(type_key[pl.ds(block * 16 + part * 2 + u, 1), :], TYPES * 8)
            rows = jnp.concatenate(picked_rows(picks[2 * (part % 2) + u], 256), axis=1)
            both.append(dot(hot, rows).reshape(TYPES, 8, WIDTH))
        row = pl.multiple_of(block * 128 + part * 16, 16)
        typed[:, pl.ds(row, 16), :] = jnp.concatenate(both, axis=1).astype(BF16)

    def leaf(i, carry):
        for stage in range(2):
            block = 2 * i + stage
            fetch(block, stage).wait()
            pick_pair(stage, 0)
            for part in range(1, 8):
                sum_pair(block, part - 1)
                pick_pair(stage, part)
            sum_pair(block, 7)
            fetch(block + 2, stage).start()
        return carry

    lax.fori_loop(0, 2, leaf, 0)
    fetch(0, 0).wait()
    fetch(0, 1).wait()

    total = out_ref[...]
    for t in range(TYPES):
        total = total + dot(typed[t], m2l[t])
    out_ref[...] = total

    pltpu.make_async_remote_copy(
        src_ref=rest, dst_ref=rest, send_sem=psend_sem, recv_sem=precv_sem, device_id=((g + 1) % 8, m), device_id_type=MESH
    ).wait_send()


def shards(density, send_list, v_src, v_type, coarse_src, coarse_type, m2l_ops, coarse_ops, m2m_ops, l2l_ops):
    dma = pltpu.SemaphoreType.DMA
    return pl.pallas_call(
        kernel,
        out_shape=jax.ShapeDtypeStruct((BOXES, WIDTH), F32),
        in_specs=[pl.BlockSpec(memory_space=pltpu.HBM)] * 10,
        out_specs=pl.BlockSpec(memory_space=pltpu.VMEM),
        scratch_shapes=[
            pltpu.VMEM((BOXES, WIDTH), BF16),
            pltpu.SMEM((1, DEVICES * GHOST), I32),
            pltpu.VMEM((SLOTS, BOXES), I32),
            pltpu.VMEM((SLOTS, BOXES), I32),
            pltpu.VMEM((SLOTS, PARENTS), I32),
            pltpu.VMEM((SLOTS, PARENTS), I32),
            pltpu.VMEM((TYPES, WIDTH, WIDTH), BF16),
            pltpu.VMEM((TYPES, WIDTH, WIDTH), BF16),
            pltpu.VMEM((8, WIDTH, WIDTH), BF16),
            pltpu.VMEM((DEVICES * GHOST, WIDTH), BF16),
            pltpu.VMEM((DEVICES * GHOST, WIDTH), BF16),
            pltpu.VMEM((PARENTS, WIDTH), BF16),
            pltpu.VMEM((8 * PARENTS, WIDTH), BF16),
            pltpu.VMEM((TYPES, BOXES, WIDTH), BF16),
            pltpu.VMEM((PARENTS, 8, WIDTH), F32),
            pltpu.VMEM(((ROWS + 2) * CHUNKS, 128), F32),
            pltpu.VMEM((256 * CHUNKS, 128), F32),
            pltpu.VMEM((256 * CHUNKS, 128), F32),
            pltpu.VMEM((256 * CHUNKS, 128), F32),
            pltpu.VMEM((256 * CHUNKS, 128), F32),
            pltpu.SMEM((SLOTS, 128), I32),
            pltpu.SMEM((SLOTS, 128), I32),
            pltpu.VMEM((SLOTS, BOXES), I32),
            pltpu.VMEM((BOXES // 8, 8 * SLOTS), F32),
            pltpu.VMEM((PARENTS // 8, 8 * SLOTS), F32),
            pltpu.VMEM((PARENTS // 8, 8 * SLOTS), F32),
            pltpu.VMEM((TYPES, PARENTS, 2 * LO), BF16),
            dma((6,)),
            dma((4,)),
            dma((2,)),
            dma,
            dma,
            dma,
            dma,
        ],
        compiler_params=pltpu.CompilerParams(
            collective_id=0, has_side_effects=True, vmem_limit_bytes=48 * 1024 * 1024
        ),
        cost_estimate=pl.CostEstimate(flops=8_000_000_000, bytes_accessed=30_000_000, transcendentals=0),
        name="far_field",
    )(density, send_list, v_src.T, v_type.T, coarse_src.T, coarse_type.T, m2l_ops, coarse_ops, m2m_ops, l2l_ops)


def solution(mesh):
    row = P(("morton", "grp"), None)
    return jax.shard_map(
        shards,
        mesh=mesh,
        in_specs=(row, row, row, row, row, row, P(), P(), P(), P()),
        out_specs=row,
        check_vma=False,
    )
```

```python
import jax
import jax.numpy as jnp
from jax import lax
from jax.experimental import pallas as pl
from jax.experimental.pallas import tpu as pltpu
from jax.sharding import PartitionSpec as P

MESH = pl.DeviceIdType.MESH
BF16 = jnp.bfloat16
F32 = jnp.float32
I32 = jnp.int32

DEVICES = 128
GHOST = 16
BOXES = 512
WIDTH = 512
TYPES = 12
SLOTS = 32
PARENTS = 64
LO = 256
KEYS = 2 * TYPES * 8
NONE = 255.0
ROWS = BOXES + DEVICES * GHOST
CHUNKS = WIDTH // 128


def dot(a, b):
    return jnp.dot(a, b, preferred_element_type=F32)


def dot_t(a, b):
    return lax.dot_general(a, b, (((1,), (1,)), ((), ())), preferred_element_type=F32)


def iota(shape, dim):
    return lax.broadcasted_iota(I32, shape, dim)


def to_lanes(values):
    n = values.shape[0]
    spread = (iota((SLOTS, 8 * SLOTS), 1) % SLOTS == iota((SLOTS, 8 * SLOTS), 0)).astype(F32).astype(BF16)
    wide = dot(values.astype(F32).astype(BF16), spread)
    own = iota((n, 8 * SLOTS), 0) % 8 == iota((n, 8 * SLOTS), 1) // SLOTS
    wide = jnp.where(own, wide, 0.0).astype(BF16)
    rows = (iota((n // 8, n), 1) // 8 == iota((n // 8, n), 0)).astype(F32).astype(BF16)
    return dot(rows, wide)


def write_keys(column, kind, key_ref, lo_ref):
    n = column.shape[0]
    hi = column // LO
    key = (hi % 2) * (TYPES * 8) + kind * 8 + iota((n, SLOTS), 0) % 8
    key_ref[...] = jnp.where(to_lanes(hi // 2) == 0.0, to_lanes(key), NONE)
    lo_ref[...] = to_lanes(column % LO)


def one_hot(row, count):
    wide = jnp.broadcast_to(row, (16, row.shape[1])).astype(BF16)
    shape = (count // 16, 16, row.shape[1])
    index = (iota(shape, 0) * 16 + iota(shape, 1)).astype(F32).astype(BF16)
    return jnp.where(wide[None] == index, jnp.ones((), BF16), jnp.zeros((), BF16)).reshape(count, row.shape[1])


def build_counts(pair, key_ref, lo_ref, count_ref):
    results = []
    for u in range(2):
        group = 2 * pair + u
        low = one_hot(lo_ref[pl.ds(group, 1), :], LO)
        results.append(dot_t(one_hot(key_ref[pl.ds(group, 1), :], KEYS), low))
    row = pl.multiple_of(pair * 16, 16)
    for half in range(2):
        first = half * (KEYS // 2)
        both = [r[first : first + KEYS // 2].reshape(TYPES, 8, LO) for r in results]
        count_ref[:, pl.ds(row, 16), half * LO : (half + 1) * LO] = jnp.concatenate(both, axis=1).astype(BF16)


def to_table(rows_ref, first, count, tab, at):
    for j in range(CHUNKS):
        part = rows_ref[first : first + count, j * 128 : (j + 1) * 128].astype(F32)
        tab[pl.ds(at * CHUNKS + j, count, stride=CHUNKS), :] = part


def pick(tab, start, picked, slot):
    picked[slot * CHUNKS : (slot + 1) * CHUNKS, :] = tab[pl.ds(start, CHUNKS), :]


def picked_rows(picked, count):
    return [picked[pl.ds(j, count, stride=CHUNKS), :].astype(BF16) for j in range(CHUNKS)]


def step_of(i):
    s = i // 32
    dy = (i // 8) % 4
    dz = (i // 2) % 4
    dc = i % 2
    dx = (s + 8 - dy - dz) % 4
    return dy, dc, dz, dx


def kernel(
    density_h, send_h, v_src_h, v_type_h, c_src_h, c_type_h, m2l_h, cops_h, m2m_h, l2l_h,
    out_ref,
    dens, send, v_src, v_type, c_src, c_type, m2l, cops, octant,
    outgoing, ghosts, parents, group, typed, from_parent, tab, pick_0, pick_1, pick_2, pick_3, start_a, start_b, scaled,
    type_key, ckey_ref, clo_ref, ccounts,
    load_sem, weight_sem, index_sem, send_sem, recv_sem, psend_sem, precv_sem,
):
    g = lax.axis_index("grp")
    m = lax.axis_index("morton")
    me = g * 16 + m
    picks = (pick_0, pick_1, pick_2, pick_3)
    my, mc, mz, mx = g // 2, g % 2, m // 4, m % 4

    loads = []
    for j, (src, dst) in enumerate(
        ((density_h, dens), (send_h, send), (v_src_h, v_src), (v_type_h, v_type), (c_src_h, c_src), (c_type_h, c_type))
    ):
        loads.append(pltpu.make_async_copy(src, dst, load_sem.at[j]))
    load_m2m = pltpu.make_async_copy(m2m_h, octant, weight_sem.at[0])
    load_cops = pltpu.make_async_copy(cops_h, cops, weight_sem.at[1])
    load_m2l = pltpu.make_async_copy(m2l_h, m2l, weight_sem.at[2])
    load_l2l = pltpu.make_async_copy(l2l_h, octant, weight_sem.at[3])
    for load in loads[:2]:
        load.start()
    load_m2m.start()
    for load in loads[2:]:
        load.start()

    barrier = pltpu.get_barrier_semaphore()

    def greet(i, carry):
        other = (me + i) % DEVICES
        pl.semaphore_signal(barrier, inc=1, device_id=(other // 16, other % 16), device_id_type=MESH)
        return carry

    lax.fori_loop(1, DEVICES, greet, 0)

    loads[0].wait()
    to_table(dens, 0, BOXES, tab, 0)
    tab[ROWS * CHUNKS : (ROWS + 2) * CHUNKS, :] = jnp.zeros((2 * CHUNKS, 128), F32)
    loads[1].wait()

    for q in range(8):
        picked = picks[q % 4]
        for s in range(256):
            pick(tab, send[0, q * 256 + s] * CHUNKS, picked, s)
        for j, part in enumerate(picked_rows(picked, 256)):
            outgoing[q * 256 : (q + 1) * 256, j * 128 : (j + 1) * 128] = part

    ghosts[pl.ds(pl.multiple_of(me * GHOST, GHOST), GHOST), :] = outgoing[pl.ds(pl.multiple_of(me * GHOST, GHOST), GHOST), :]

    pl.semaphore_wait(barrier, DEVICES - 1)

    def send_rows(i, carry):
        dy, dc, dz, dx = step_of(i)
        g2 = ((my + dy) % 4) * 2 + (mc + dc) % 2
        m2 = ((mz + dz) % 4) * 4 + (mx + dx) % 4
        there = pl.multiple_of((g2 * 16 + m2) * GHOST, GHOST)
        pltpu.make_async_remote_copy(
            src_ref=outgoing.at[pl.ds(there, GHOST)],
            dst_ref=ghosts.at[pl.ds(pl.multiple_of(me * GHOST, GHOST), GHOST)],
            send_sem=send_sem, recv_sem=recv_sem.at[i // 32],
            device_id=(g2, m2), device_id_type=MESH,
        ).start()
        return carry

    lax.fori_loop(1, 64, send_rows, 0)

    r = iota((BOXES, BOXES), 0)
    order = (iota((BOXES, BOXES), 1) == (r % PARENTS) * 8 + r // PARENTS).astype(F32).astype(BF16)
    by_octant = dot(order, dens[...]).astype(BF16)
    load_m2m.wait()
    total = dot(by_octant[0:PARENTS], octant[0])
    for k in range(1, 8):
        total = total + dot(by_octant[k * PARENTS : (k + 1) * PARENTS], octant[k])
    mine = total.astype(BF16)
    parents[...] = mine
    my_rows = pl.ds(pl.multiple_of(g * PARENTS, PARENTS), PARENTS)
    group[my_rows, :] = mine
    for i in range(1, 8):
        pltpu.make_async_remote_copy(
            src_ref=parents, dst_ref=group.at[my_rows], send_sem=psend_sem, recv_sem=precv_sem,
            device_id=((g + i) % 8, m), device_id_type=MESH,
        ).start()
    load_l2l.start()
    load_cops.start()
    load_m2l.start()
    lax.fori_loop(64, DEVICES, send_rows, 0)

    for load in loads[2:]:
        load.wait()
    scaled[...] = v_src[...] * CHUNKS
    kinds = v_type[...].T
    type_key[...] = to_lanes(kinds * 8 + iota((BOXES, SLOTS), 0) % 8)
    write_keys(c_src[...].T, c_type[...].T, ckey_ref, clo_ref)

    def build_coarse(pair, carry):
        build_counts(pair, ckey_ref, clo_ref, ccounts)
        return carry

    lax.fori_loop(0, 4, build_coarse, 0)
    rest = group.at[pl.ds(0, 7 * PARENTS)]
    pltpu.make_async_remote_copy(
        src_ref=rest, dst_ref=rest, send_sem=psend_sem, recv_sem=precv_sem, device_id=((g + 1) % 8, m), device_id_type=MESH
    ).wait_recv()
    load_cops.wait()

    def coarse_step(t, total):
        summed = dot(ccounts[t], group[...]).astype(BF16)
        return total + dot(summed, cops[t])

    coarse = lax.fori_loop(0, TYPES, coarse_step, jnp.zeros((PARENTS, WIDTH), F32)).astype(BF16)
    load_l2l.wait()
    for k in range(8):
        from_parent[:, k, :] = dot(coarse, octant[k])
    out_ref[...] = from_parent[...].reshape(BOXES, WIDTH)

    def fetch(block, stage):
        first = pl.multiple_of(jnp.minimum(block, 3) * 128, 128)
        return pltpu.make_async_copy(scaled.at[:, pl.ds(first, 128)], (start_a, start_b)[stage], index_sem.at[stage])

    fetch(0, 0).start()
    fetch(1, 1).start()
    load_m2l.wait()
    def unpack(i, carry):
        dy, dc, dz, dx = step_of(i)
        sender = (((my + 4 - dy) % 4) * 2 + (mc + 2 - dc) % 2) * 16 + ((mz + 4 - dz) % 4) * 4 + (mx + 4 - dx) % 4
        first = pl.multiple_of(sender * GHOST, GHOST)
        for j in range(CHUNKS):
            part = ghosts[pl.ds(first, GHOST), j * 128 : (j + 1) * 128].astype(F32)
            tab[pl.ds((BOXES + first) * CHUNKS + j, GHOST, stride=CHUNKS), :] = part
        return carry

    for part in range(4):
        came = ghosts.at[pl.ds(0, 32 * GHOST if part else 31 * GHOST)]
        pltpu.make_async_remote_copy(
            src_ref=came, dst_ref=came, send_sem=send_sem, recv_sem=recv_sem.at[part],
            device_id=((g + 1) % 8, m), device_id_type=MESH,
        ).wait_recv()
        lax.fori_loop(part * 32, part * 32 + 32, unpack, 0)

    def pick_pair(stage, part):
        for u in range(2):
            for s in range(256):
                column = part * 16 + u * 8 + s // SLOTS
                pick(tab, (start_a, start_b)[stage][s % SLOTS, column], picks[2 * (part % 2) + u], s)

    def sum_pair(block, part):
        both = []
        for u in range(2):
            hot = one_hot(type_key[pl.ds(block * 16 + part * 2 + u, 1), :], TYPES * 8)
            rows = jnp.concatenate(picked_rows(picks[2 * (part % 2) + u], 256), axis=1)
            both.append(dot(hot, rows).reshape(TYPES, 8, WIDTH))
        row = pl.multiple_of(block * 128 + part * 16, 16)
        typed[:, pl.ds(row, 16), :] = jnp.concatenate(both, axis=1).astype(BF16)

    def leaf(i, carry):
        for stage in range(2):
            block = 2 * i + stage
            fetch(block, stage).wait()
            pick_pair(stage, 0)
            for part in range(1, 8):
                sum_pair(block, part - 1)
                pick_pair(stage, part)
            sum_pair(block, 7)
            fetch(block + 2, stage).start()
        return carry

    lax.fori_loop(0, 2, leaf, 0)
    fetch(0, 0).wait()
    fetch(0, 1).wait()

    total = out_ref[...]
    for t in range(TYPES):
        total = total + dot(typed[t], m2l[t])
    out_ref[...] = total

    went = outgoing.at[pl.ds(0, (DEVICES - 1) * GHOST)]
    pltpu.make_async_remote_copy(
        src_ref=went, dst_ref=went, send_sem=send_sem, recv_sem=recv_sem.at[0],
        device_id=((g + 1) % 8, m), device_id_type=MESH,
    ).wait_send()
    pltpu.make_async_remote_copy(
        src_ref=rest, dst_ref=rest, send_sem=psend_sem, recv_sem=precv_sem, device_id=((g + 1) % 8, m), device_id_type=MESH
    ).wait_send()


def shards(density, send_list, v_src, v_type, coarse_src, coarse_type, m2l_ops, coarse_ops, m2m_ops, l2l_ops):
    dma = pltpu.SemaphoreType.DMA
    return pl.pallas_call(
        kernel,
        out_shape=jax.ShapeDtypeStruct((BOXES, WIDTH), F32),
        in_specs=[pl.BlockSpec(memory_space=pltpu.HBM)] * 10,
        out_specs=pl.BlockSpec(memory_space=pltpu.VMEM),
        scratch_shapes=[
            pltpu.VMEM((BOXES, WIDTH), BF16),
            pltpu.SMEM((1, DEVICES * GHOST), I32),
            pltpu.VMEM((SLOTS, BOXES), I32),
            pltpu.VMEM((SLOTS, BOXES), I32),
            pltpu.VMEM((SLOTS, PARENTS), I32),
            pltpu.VMEM((SLOTS, PARENTS), I32),
            pltpu.VMEM((TYPES, WIDTH, WIDTH), BF16),
            pltpu.VMEM((TYPES, WIDTH, WIDTH), BF16),
            pltpu.VMEM((8, WIDTH, WIDTH), BF16),
            pltpu.VMEM((DEVICES * GHOST, WIDTH), BF16),
            pltpu.VMEM((DEVICES * GHOST, WIDTH), BF16),
            pltpu.VMEM((PARENTS, WIDTH), BF16),
            pltpu.VMEM((8 * PARENTS, WIDTH), BF16),
            pltpu.VMEM((TYPES, BOXES, WIDTH), BF16),
            pltpu.VMEM((PARENTS, 8, WIDTH), F32),
            pltpu.VMEM(((ROWS + 2) * CHUNKS, 128), F32),
            pltpu.VMEM((256 * CHUNKS, 128), F32),
            pltpu.VMEM((256 * CHUNKS, 128), F32),
            pltpu.VMEM((256 * CHUNKS, 128), F32),
            pltpu.VMEM((256 * CHUNKS, 128), F32),
            pltpu.SMEM((SLOTS, 128), I32),
            pltpu.SMEM((SLOTS, 128), I32),
            pltpu.VMEM((SLOTS, BOXES), I32),
            pltpu.VMEM((BOXES // 8, 8 * SLOTS), F32),
            pltpu.VMEM((PARENTS // 8, 8 * SLOTS), F32),
            pltpu.VMEM((PARENTS // 8, 8 * SLOTS), F32),
            pltpu.VMEM((TYPES, PARENTS, 2 * LO), BF16),
            dma((6,)),
            dma((4,)),
            dma((2,)),
            dma,
            dma((4,)),
            dma,
            dma,
        ],
        compiler_params=pltpu.CompilerParams(
            collective_id=0, has_side_effects=True, vmem_limit_bytes=56 * 1024 * 1024
        ),
        cost_estimate=pl.CostEstimate(flops=8_000_000_000, bytes_accessed=30_000_000, transcendentals=0),
        name="far_field",
    )(density, send_list, v_src.T, v_type.T, coarse_src.T, coarse_type.T, m2l_ops, coarse_ops, m2m_ops, l2l_ops)


def solution(mesh):
    row = P(("morton", "grp"), None)
    return jax.shard_map(
        shards,
        mesh=mesh,
        in_specs=(row, row, row, row, row, row, P(), P(), P(), P()),
        out_specs=row,
        check_vma=False,
    )
```

```python
import jax
import jax.numpy as jnp
from jax import lax
from jax.experimental import pallas as pl
from jax.experimental.pallas import tpu as pltpu
from jax.sharding import PartitionSpec as P

MESH = pl.DeviceIdType.MESH
BF16 = jnp.bfloat16
F32 = jnp.float32
I32 = jnp.int32

DEVICES = 128
GHOST = 16
BOXES = 512
WIDTH = 512
TYPES = 12
SLOTS = 32
PARENTS = 64
LO = 256
KEYS = 2 * TYPES * 8
NONE = 255.0
ROWS = BOXES + DEVICES * GHOST
CHUNKS = WIDTH // 128


def dot(a, b):
    return jnp.dot(a, b, preferred_element_type=F32)


def dot_t(a, b):
    return lax.dot_general(a, b, (((1,), (1,)), ((), ())), preferred_element_type=F32)


def iota(shape, dim):
    return lax.broadcasted_iota(I32, shape, dim)


def to_lanes(values):
    n = values.shape[0]
    spread = (iota((SLOTS, 8 * SLOTS), 1) % SLOTS == iota((SLOTS, 8 * SLOTS), 0)).astype(F32).astype(BF16)
    wide = dot(values.astype(F32).astype(BF16), spread)
    own = iota((n, 8 * SLOTS), 0) % 8 == iota((n, 8 * SLOTS), 1) // SLOTS
    wide = jnp.where(own, wide, 0.0).astype(BF16)
    rows = (iota((n // 8, n), 1) // 8 == iota((n // 8, n), 0)).astype(F32).astype(BF16)
    return dot(rows, wide)


def write_keys(column, kind, parts, key_ref, lo_ref):
    n = column.shape[0]
    hi = column // LO
    key = to_lanes((hi % 2) * (TYPES * 8) + kind * 8 + iota((n, SLOTS), 0) % 8)
    part_row = to_lanes(hi // 2)
    lo_ref[...] = to_lanes(column % LO)
    for part in range(parts):
        key_ref[part] = jnp.where(part_row == float(part), key, NONE)


def one_hot(row, count):
    wide = jnp.broadcast_to(row, (16, row.shape[1])).astype(BF16)
    shape = (count // 16, 16, row.shape[1])
    index = (iota(shape, 0) * 16 + iota(shape, 1)).astype(F32).astype(BF16)
    return jnp.where(wide[None] == index, jnp.ones((), BF16), jnp.zeros((), BF16)).reshape(count, row.shape[1])


def build_counts(pair, parts, key_ref, lo_ref, count_ref):
    results = []
    for u in range(2):
        group = 2 * pair + u
        low = one_hot(lo_ref[pl.ds(group, 1), :], LO)
        hot = jnp.concatenate([one_hot(key_ref[part, pl.ds(group, 1), :], KEYS) for part in range(parts)], axis=0)
        results.append(dot_t(hot, low))
    row = pl.multiple_of(pair * 16, 16)
    for part in range(parts):
        for half in range(2):
            first = part * KEYS + half * (KEYS // 2)
            both = [r[first : first + KEYS // 2].reshape(TYPES, 8, LO) for r in results]
            count_ref[part, :, pl.ds(row, 16), half * LO : (half + 1) * LO] = jnp.concatenate(both, axis=1).astype(BF16)


def to_table(rows_ref, first, count, tab, at):
    for j in range(CHUNKS):
        part = rows_ref[first : first + count, j * 128 : (j + 1) * 128].astype(F32)
        tab[pl.ds(at * CHUNKS + j, count, stride=CHUNKS), :] = part


def pick(tab, start, picked, slot):
    picked[slot * CHUNKS : (slot + 1) * CHUNKS, :] = tab[pl.ds(start, CHUNKS), :]


def picked_rows(picked, count):
    return [picked[pl.ds(j, count, stride=CHUNKS), :].astype(BF16) for j in range(CHUNKS)]


def step_of(i):
    s = i // 32
    dy = (i // 8) % 4
    dz = (i // 2) % 4
    dc = i % 2
    dx = (s + 8 - dy - dz) % 4
    return dy, dc, dz, dx


def kernel(
    density_h, send_h, v_src_h, v_type_h, c_src_h, c_type_h, m2l_h, cops_h, m2m_h, l2l_h,
    out_ref,
    dens, send, v_src, v_type, c_src, c_type, m2l, cops, octant,
    outgoing, ghosts, parents, group, typed, from_parent, tab, pick_0, pick_1, pick_2, pick_3, start_a, start_b, scaled,
    type_key, ckey_ref, clo_ref, ccounts, key_ref, lo_ref, counts, partial,
    load_sem, weight_sem, index_sem, send_sem, recv_sem, psend_sem, precv_sem,
):
    g = lax.axis_index("grp")
    m = lax.axis_index("morton")
    me = g * 16 + m
    picks = (pick_0, pick_1, pick_2, pick_3)
    my, mc, mz, mx = g // 2, g % 2, m // 4, m % 4

    loads = []
    for j, (src, dst) in enumerate(
        ((density_h, dens), (send_h, send), (v_src_h, v_src), (v_type_h, v_type), (c_src_h, c_src), (c_type_h, c_type))
    ):
        loads.append(pltpu.make_async_copy(src, dst, load_sem.at[j]))
    load_m2m = pltpu.make_async_copy(m2m_h, octant, weight_sem.at[0])
    load_cops = pltpu.make_async_copy(cops_h, cops, weight_sem.at[1])
    load_m2l = pltpu.make_async_copy(m2l_h, m2l, weight_sem.at[2])
    load_l2l = pltpu.make_async_copy(l2l_h, octant, weight_sem.at[3])
    for load in loads[:2]:
        load.start()
    load_m2m.start()
    for load in loads[2:]:
        load.start()

    barrier = pltpu.get_barrier_semaphore()

    def greet(i, carry):
        other = (me + i) % DEVICES
        pl.semaphore_signal(barrier, inc=1, device_id=(other // 16, other % 16), device_id_type=MESH)
        return carry

    lax.fori_loop(1, DEVICES, greet, 0)

    loads[0].wait()
    to_table(dens, 0, BOXES, tab, 0)
    tab[ROWS * CHUNKS : (ROWS + 2) * CHUNKS, :] = jnp.zeros((2 * CHUNKS, 128), F32)
    loads[1].wait()

    for q in range(8):
        picked = picks[q % 4]
        for s in range(256):
            pick(tab, send[0, q * 256 + s] * CHUNKS, picked, s)
        for j, part in enumerate(picked_rows(picked, 256)):
            outgoing[q * 256 : (q + 1) * 256, j * 128 : (j + 1) * 128] = part

    ghosts[0:GHOST, :] = outgoing[pl.ds(pl.multiple_of(me * GHOST, GHOST), GHOST), :]

    pl.semaphore_wait(barrier, DEVICES - 1)

    def send_rows(i, carry):
        dy, dc, dz, dx = step_of(i)
        g2 = ((my + dy) % 4) * 2 + (mc + dc) % 2
        m2 = ((mz + dz) % 4) * 4 + (mx + dx) % 4
        there = pl.multiple_of((g2 * 16 + m2) * GHOST, GHOST)
        pltpu.make_async_remote_copy(
            src_ref=outgoing.at[pl.ds(there, GHOST)],
            dst_ref=ghosts.at[pl.ds(pl.multiple_of(i * GHOST, GHOST), GHOST)],
            send_sem=send_sem, recv_sem=recv_sem.at[i // 32],
            device_id=(g2, m2), device_id_type=MESH,
        ).start()
        return carry

    lax.fori_loop(1, 64, send_rows, 0)

    r = iota((BOXES, BOXES), 0)
    order = (iota((BOXES, BOXES), 1) == (r % PARENTS) * 8 + r // PARENTS).astype(F32).astype(BF16)
    by_octant = dot(order, dens[...]).astype(BF16)
    load_m2m.wait()
    total = dot(by_octant[0:PARENTS], octant[0])
    for k in range(1, 8):
        total = total + dot(by_octant[k * PARENTS : (k + 1) * PARENTS], octant[k])
    mine = total.astype(BF16)
    parents[...] = mine
    my_rows = pl.ds(pl.multiple_of(g * PARENTS, PARENTS), PARENTS)
    group[my_rows, :] = mine
    for i in range(1, 8):
        pltpu.make_async_remote_copy(
            src_ref=parents, dst_ref=group.at[my_rows], send_sem=psend_sem, recv_sem=precv_sem,
            device_id=((g + i) % 8, m), device_id_type=MESH,
        ).start()
    load_l2l.start()
    load_cops.start()
    load_m2l.start()
    lax.fori_loop(64, DEVICES, send_rows, 0)

    for load in loads[2:]:
        load.wait()
    source = v_src[...]
    beyond = jnp.maximum(source - BOXES, 0)
    sender = beyond // GHOST
    dx = (mx + 4 - sender % 4) % 4
    dz = (mz + 4 - (sender // 4) % 4) % 4
    dc = (mc + 2 - (sender // 16) % 2) % 2
    dy = (my + 4 - (sender // 32) % 4) % 4
    place = ((dx + dy + dz) % 4) * 32 + dy * 8 + dz * 2 + dc
    moved = BOXES + place * GHOST + beyond % GHOST
    column = jnp.where(source < BOXES, source, jnp.where(source < ROWS, moved, ROWS))
    scaled[...] = column * CHUNKS
    kinds = v_type[...].T
    type_key[...] = to_lanes(kinds * 8 + iota((BOXES, SLOTS), 0) % 8)
    write_keys(column[:, 0:128].T, kinds[0:128], 5, key_ref, lo_ref)
    write_keys(c_src[...].T, c_type[...].T, 1, ckey_ref, clo_ref)

    def build_leaf(pair, carry):
        build_counts(pair, 5, key_ref, lo_ref, counts)
        return carry

    lax.fori_loop(0, 8, build_leaf, 0)

    def product(part, rows):
        return dot(counts[part].reshape(TYPES * 128, 2 * LO), rows).reshape(TYPES, 128, WIDTH)

    partial[...] = product(0, dens[...])

    def build_coarse(pair, carry):
        build_counts(pair, 1, ckey_ref, clo_ref, ccounts)
        return carry

    lax.fori_loop(0, 4, build_coarse, 0)
    rest = group.at[pl.ds(0, 7 * PARENTS)]
    pltpu.make_async_remote_copy(
        src_ref=rest, dst_ref=rest, send_sem=psend_sem, recv_sem=precv_sem, device_id=((g + 1) % 8, m), device_id_type=MESH
    ).wait_recv()
    load_cops.wait()

    def coarse_step(t, total):
        summed = dot(ccounts[0, t], group[...]).astype(BF16)
        return total + dot(summed, cops[t])

    coarse = lax.fori_loop(0, TYPES, coarse_step, jnp.zeros((PARENTS, WIDTH), F32)).astype(BF16)
    load_l2l.wait()
    for k in range(8):
        from_parent[:, k, :] = dot(coarse, octant[k])
    out_ref[...] = from_parent[...].reshape(BOXES, WIDTH)

    def fetch(block, stage):
        first = pl.multiple_of(jnp.minimum(block, 3) * 128, 128)
        return pltpu.make_async_copy(scaled.at[:, pl.ds(first, 128)], (start_a, start_b)[stage], index_sem.at[stage])

    fetch(1, 0).start()
    fetch(1, 1).start()
    load_m2l.wait()
    for part in range(4):
        came = ghosts.at[pl.ds(0, (32 if part else 31) * GHOST)]
        pltpu.make_async_remote_copy(
            src_ref=came, dst_ref=came, send_sem=send_sem, recv_sem=recv_sem.at[part],
            device_id=((g + 1) % 8, m), device_id_type=MESH,
        ).wait_recv()
        to_table(ghosts, part * 512, 512, tab, BOXES + part * 512)
        added = partial[...] + product(part + 1, ghosts[part * 512 : (part + 1) * 512, :])
        if part < 3:
            partial[...] = added
        else:
            typed[:, 0:128, :] = added.astype(BF16)

    def pick_pair(stage, part):
        for u in range(2):
            for s in range(256):
                column = part * 16 + u * 8 + s // SLOTS
                pick(tab, (start_a, start_b)[stage][s % SLOTS, column], picks[2 * (part % 2) + u], s)

    def sum_pair(block, part):
        both = []
        for u in range(2):
            hot = one_hot(type_key[pl.ds(block * 16 + part * 2 + u, 1), :], TYPES * 8)
            rows = jnp.concatenate(picked_rows(picks[2 * (part % 2) + u], 256), axis=1)
            both.append(dot(hot, rows).reshape(TYPES, 8, WIDTH))
        row = pl.multiple_of(block * 128 + part * 16, 16)
        typed[:, pl.ds(row, 16), :] = jnp.concatenate(both, axis=1).astype(BF16)

    def leaf(block, carry):
        for part in range(8):
            stage = part // 4
            if part % 4 == 0:
                fetch(block, stage).wait()
            pick_pair(stage, part)
            if part % 4 == 3:
                fetch(block + 1, stage).start()
            if part:
                sum_pair(block, part - 1)
        sum_pair(block, 7)
        return carry

    lax.fori_loop(1, 4, leaf, 0)
    fetch(0, 0).wait()
    fetch(0, 1).wait()

    total = out_ref[...]
    for t in range(TYPES):
        total = total + dot(typed[t], m2l[t])
    out_ref[...] = total

    went = outgoing.at[pl.ds(0, (DEVICES - 1) * GHOST)]
    pltpu.make_async_remote_copy(
        src_ref=went, dst_ref=went, send_sem=send_sem, recv_sem=recv_sem.at[0],
        device_id=((g + 1) % 8, m), device_id_type=MESH,
    ).wait_send()
    pltpu.make_async_remote_copy(
        src_ref=rest, dst_ref=rest, send_sem=psend_sem, recv_sem=precv_sem, device_id=((g + 1) % 8, m), device_id_type=MESH
    ).wait_send()


def shards(density, send_list, v_src, v_type, coarse_src, coarse_type, m2l_ops, coarse_ops, m2m_ops, l2l_ops):
    dma = pltpu.SemaphoreType.DMA
    return pl.pallas_call(
        kernel,
        out_shape=jax.ShapeDtypeStruct((BOXES, WIDTH), F32),
        in_specs=[pl.BlockSpec(memory_space=pltpu.HBM)] * 10,
        out_specs=pl.BlockSpec(memory_space=pltpu.VMEM),
        scratch_shapes=[
            pltpu.VMEM((BOXES, WIDTH), BF16),
            pltpu.SMEM((1, DEVICES * GHOST), I32),
            pltpu.VMEM((SLOTS, BOXES), I32),
            pltpu.VMEM((SLOTS, BOXES), I32),
            pltpu.VMEM((SLOTS, PARENTS), I32),
            pltpu.VMEM((SLOTS, PARENTS), I32),
            pltpu.VMEM((TYPES, WIDTH, WIDTH), BF16),
            pltpu.VMEM((TYPES, WIDTH, WIDTH), BF16),
            pltpu.VMEM((8, WIDTH, WIDTH), BF16),
            pltpu.VMEM((DEVICES * GHOST, WIDTH), BF16),
            pltpu.VMEM((DEVICES * GHOST, WIDTH), BF16),
            pltpu.VMEM((PARENTS, WIDTH), BF16),
            pltpu.VMEM((8 * PARENTS, WIDTH), BF16),
            pltpu.VMEM((TYPES, BOXES, WIDTH), BF16),
            pltpu.VMEM((PARENTS, 8, WIDTH), F32),
            pltpu.VMEM(((ROWS + 2) * CHUNKS, 128), F32),
            pltpu.VMEM((256 * CHUNKS, 128), F32),
            pltpu.VMEM((256 * CHUNKS, 128), F32),
            pltpu.VMEM((256 * CHUNKS, 128), F32),
            pltpu.VMEM((256 * CHUNKS, 128), F32),
            pltpu.SMEM((SLOTS, 128), I32),
            pltpu.SMEM((SLOTS, 128), I32),
            pltpu.VMEM((SLOTS, BOXES), I32),
            pltpu.VMEM((BOXES // 8, 8 * SLOTS), F32),
            pltpu.VMEM((1, PARENTS // 8, 8 * SLOTS), F32),
            pltpu.VMEM((PARENTS // 8, 8 * SLOTS), F32),
            pltpu.VMEM((1, TYPES, PARENTS, 2 * LO), BF16),
            pltpu.VMEM((5, 16, 8 * SLOTS), F32),
            pltpu.VMEM((16, 8 * SLOTS), F32),
            pltpu.VMEM((5, TYPES, 128, 2 * LO), BF16),
            pltpu.VMEM((TYPES, 128, WIDTH), F32),
            dma((6,)),
            dma((4,)),
            dma((2,)),
            dma,
            dma((4,)),
            dma,
            dma,
        ],
        compiler_params=pltpu.CompilerParams(
            collective_id=0, has_side_effects=True, vmem_limit_bytes=60 * 1024 * 1024
        ),
        cost_estimate=pl.CostEstimate(flops=8_000_000_000, bytes_accessed=30_000_000, transcendentals=0),
        name="far_field",
    )(density, send_list, v_src.T, v_type.T, coarse_src.T, coarse_type.T, m2l_ops, coarse_ops, m2m_ops, l2l_ops)


def solution(mesh):
    row = P(("morton", "grp"), None)
    return jax.shard_map(
        shards,
        mesh=mesh,
        in_specs=(row, row, row, row, row, row, P(), P(), P(), P()),
        out_specs=row,
        check_vma=False,
    )
```

```python
import jax
import jax.numpy as jnp
from jax import lax
from jax.experimental import pallas as pl
from jax.experimental.pallas import tpu as pltpu
from jax.sharding import PartitionSpec as P

MESH = pl.DeviceIdType.MESH
BF16 = jnp.bfloat16
F32 = jnp.float32
I32 = jnp.int32

DEVICES = 128
GHOST = 16
BOXES = 512
WIDTH = 512
TYPES = 12
SLOTS = 32
PARENTS = 64
LO = 256
KEYS = 2 * TYPES * 8
NONE = 255.0
ROWS = BOXES + DEVICES * GHOST
CHUNKS = WIDTH // 128


def dot(a, b):
    return jnp.dot(a, b, preferred_element_type=F32)


def dot_t(a, b):
    return lax.dot_general(a, b, (((1,), (1,)), ((), ())), preferred_element_type=F32)


def iota(shape, dim):
    return lax.broadcasted_iota(I32, shape, dim)


def to_lanes(values):
    n = values.shape[0]
    spread = (iota((SLOTS, 8 * SLOTS), 1) % SLOTS == iota((SLOTS, 8 * SLOTS), 0)).astype(F32).astype(BF16)
    wide = dot(values.astype(F32).astype(BF16), spread)
    own = iota((n, 8 * SLOTS), 0) % 8 == iota((n, 8 * SLOTS), 1) // SLOTS
    wide = jnp.where(own, wide, 0.0).astype(BF16)
    rows = (iota((n // 8, n), 1) // 8 == iota((n // 8, n), 0)).astype(F32).astype(BF16)
    return dot(rows, wide)


def write_keys(column, kind, parts, key_ref, lo_ref):
    n = column.shape[0]
    hi = column // LO
    key = to_lanes((hi % 2) * (TYPES * 8) + kind * 8 + iota((n, SLOTS), 0) % 8)
    part_row = to_lanes(hi // 2)
    lo_ref[...] = to_lanes(column % LO)
    for part in range(parts):
        key_ref[part] = jnp.where(part_row == float(part), key, NONE)


def one_hot(row, count):
    wide = jnp.broadcast_to(row, (16, row.shape[1])).astype(BF16)
    shape = (count // 16, 16, row.shape[1])
    index = (iota(shape, 0) * 16 + iota(shape, 1)).astype(F32).astype(BF16)
    return jnp.where(wide[None] == index, jnp.ones((), BF16), jnp.zeros((), BF16)).reshape(count, row.shape[1])


def build_counts(pair, parts, key_ref, lo_ref, count_ref):
    results = []
    for u in range(2):
        group = 2 * pair + u
        low = one_hot(lo_ref[pl.ds(group, 1), :], LO)
        hot = jnp.concatenate([one_hot(key_ref[part, pl.ds(group, 1), :], KEYS) for part in range(parts)], axis=0)
        results.append(dot_t(hot, low))
    row = pl.multiple_of(pair * 16, 16)
    for part in range(parts):
        for half in range(2):
            first = part * KEYS + half * (KEYS // 2)
            both = [r[first : first + KEYS // 2].reshape(TYPES, 8, LO) for r in results]
            count_ref[part, :, pl.ds(row, 16), half * LO : (half + 1) * LO] = jnp.concatenate(both, axis=1).astype(BF16)


def to_table(rows_ref, first, count, tab, at):
    for j in range(CHUNKS):
        part = rows_ref[first : first + count, j * 128 : (j + 1) * 128].astype(F32)
        tab[pl.ds(at * CHUNKS + j, count, stride=CHUNKS), :] = part


def pick(tab, start, picked, slot):
    picked[slot * CHUNKS : (slot + 1) * CHUNKS, :] = tab[pl.ds(start, CHUNKS), :]


def picked_rows(picked, count):
    return [picked[pl.ds(j, count, stride=CHUNKS), :].astype(BF16) for j in range(CHUNKS)]


def step_of(i):
    s = i // 32
    dy = (i // 8) % 4
    dz = (i // 2) % 4
    dc = i % 2
    dx = (s + 8 - dy - dz) % 4
    return dy, dc, dz, dx


def kernel(
    density_h, send_h, v_src_h, v_type_h, c_src_h, c_type_h, m2l_h, cops_h, m2m_h, l2l_h,
    out_ref,
    dens, send, v_src, v_type, c_src, c_type, m2l, cops, octant,
    outgoing, ghosts, parents, group, typed, from_parent, tab, pick_0, pick_1, pick_2, pick_3, start_a, start_b, scaled,
    type_key, ckey_ref, clo_ref, ccounts, key_ref, lo_ref, counts, partial,
    load_sem, weight_sem, index_sem, send_sem, recv_sem, psend_sem, precv_sem,
):
    g = lax.axis_index("grp")
    m = lax.axis_index("morton")
    me = g * 16 + m
    picks = (pick_0, pick_1, pick_2, pick_3)
    my, mc, mz, mx = g // 2, g % 2, m // 4, m % 4

    loads = []
    for j, (src, dst) in enumerate(
        ((density_h, dens), (send_h, send), (v_src_h, v_src), (v_type_h, v_type), (c_src_h, c_src), (c_type_h, c_type))
    ):
        loads.append(pltpu.make_async_copy(src, dst, load_sem.at[j]))
    load_m2m = pltpu.make_async_copy(m2m_h, octant, weight_sem.at[0])
    load_cops = pltpu.make_async_copy(cops_h, cops, weight_sem.at[1])
    load_m2l = pltpu.make_async_copy(m2l_h, m2l, weight_sem.at[2])
    load_l2l = pltpu.make_async_copy(l2l_h, octant, weight_sem.at[3])
    for load in loads[:2]:
        load.start()
    load_m2m.start()
    for load in loads[2:]:
        load.start()

    barrier = pltpu.get_barrier_semaphore()

    def greet(i, carry):
        other = (me + i) % DEVICES
        pl.semaphore_signal(barrier, inc=1, device_id=(other // 16, other % 16), device_id_type=MESH)
        return carry

    lax.fori_loop(1, DEVICES, greet, 0)

    loads[0].wait()
    to_table(dens, 0, BOXES, tab, 0)
    tab[ROWS * CHUNKS : (ROWS + 2) * CHUNKS, :] = jnp.zeros((2 * CHUNKS, 128), F32)
    loads[1].wait()

    for q in range(8):
        picked = picks[q % 4]
        for s in range(256):
            pick(tab, send[0, q * 256 + s] * CHUNKS, picked, s)
        for j, part in enumerate(picked_rows(picked, 256)):
            outgoing[q * 256 : (q + 1) * 256, j * 128 : (j + 1) * 128] = part

    ghosts[0:GHOST, :] = outgoing[pl.ds(pl.multiple_of(me * GHOST, GHOST), GHOST), :]

    pl.semaphore_wait(barrier, DEVICES - 1)

    def send_rows(i, carry):
        dy, dc, dz, dx = step_of(i)
        g2 = ((my + dy) % 4) * 2 + (mc + dc) % 2
        m2 = ((mz + dz) % 4) * 4 + (mx + dx) % 4
        there = pl.multiple_of((g2 * 16 + m2) * GHOST, GHOST)
        pltpu.make_async_remote_copy(
            src_ref=outgoing.at[pl.ds(there, GHOST)],
            dst_ref=ghosts.at[pl.ds(pl.multiple_of(i * GHOST, GHOST), GHOST)],
            send_sem=send_sem, recv_sem=recv_sem.at[i // 32],
            device_id=(g2, m2), device_id_type=MESH,
        ).start()
        return carry

    lax.fori_loop(1, 64, send_rows, 0)

    r = iota((BOXES, BOXES), 0)
    order = (iota((BOXES, BOXES), 1) == (r % PARENTS) * 8 + r // PARENTS).astype(F32).astype(BF16)
    by_octant = dot(order, dens[...]).astype(BF16)
    load_m2m.wait()
    total = dot(by_octant[0:PARENTS], octant[0])
    for k in range(1, 8):
        total = total + dot(by_octant[k * PARENTS : (k + 1) * PARENTS], octant[k])
    mine = total.astype(BF16)
    parents[...] = mine
    my_rows = pl.ds(pl.multiple_of(g * PARENTS, PARENTS), PARENTS)
    group[my_rows, :] = mine
    for i in range(1, 8):
        pltpu.make_async_remote_copy(
            src_ref=parents, dst_ref=group.at[my_rows], send_sem=psend_sem, recv_sem=precv_sem,
            device_id=((g + i) % 8, m), device_id_type=MESH,
        ).start()
    load_l2l.start()
    load_cops.start()
    load_m2l.start()

    for load in loads[2:]:
        load.wait()
    source = v_src[...]
    beyond = jnp.maximum(source - BOXES, 0)
    sender = beyond // GHOST
    dx = (mx + 4 - sender % 4) % 4
    dz = (mz + 4 - (sender // 4) % 4) % 4
    dc = (mc + 2 - (sender // 16) % 2) % 2
    dy = (my + 4 - (sender // 32) % 4) % 4
    place = ((dx + dy + dz) % 4) * 32 + dy * 8 + dz * 2 + dc
    moved = BOXES + place * GHOST + beyond % GHOST
    column = jnp.where(source < BOXES, source, jnp.where(source < ROWS, moved, ROWS))
    scaled[...] = column * CHUNKS
    kinds = v_type[...].T
    type_key[...] = to_lanes(kinds * 8 + iota((BOXES, SLOTS), 0) % 8)
    write_keys(column[:, 0:128].T, kinds[0:128], 5, key_ref, lo_ref)
    write_keys(c_src[...].T, c_type[...].T, 1, ckey_ref, clo_ref)

    def build_leaf(pair, carry):
        for j in range(8):
            send_rows(64 + pair * 8 + j, 0)
        build_counts(pair, 5, key_ref, lo_ref, counts)
        return carry

    lax.fori_loop(0, 8, build_leaf, 0)

    def product(part, rows):
        return dot(counts[part].reshape(TYPES * 128, 2 * LO), rows).reshape(TYPES, 128, WIDTH)

    partial[...] = product(0, dens[...])

    def build_coarse(pair, carry):
        build_counts(pair, 1, ckey_ref, clo_ref, ccounts)
        return carry

    lax.fori_loop(0, 4, build_coarse, 0)
    rest = group.at[pl.ds(0, 7 * PARENTS)]
    pltpu.make_async_remote_copy(
        src_ref=rest, dst_ref=rest, send_sem=psend_sem, recv_sem=precv_sem, device_id=((g + 1) % 8, m), device_id_type=MESH
    ).wait_recv()
    load_cops.wait()

    def coarse_step(t, total):
        summed = dot(ccounts[0, t], group[...]).astype(BF16)
        return total + dot(summed, cops[t])

    coarse = lax.fori_loop(0, TYPES, coarse_step, jnp.zeros((PARENTS, WIDTH), F32)).astype(BF16)
    load_l2l.wait()
    for k in range(8):
        from_parent[:, k, :] = dot(coarse, octant[k])
    out_ref[...] = from_parent[...].reshape(BOXES, WIDTH)

    def fetch(block, stage):
        first = pl.multiple_of(jnp.minimum(block, 3) * 128, 128)
        return pltpu.make_async_copy(scaled.at[:, pl.ds(first, 128)], (start_a, start_b)[stage], index_sem.at[stage])

    fetch(1, 0).start()
    fetch(1, 1).start()
    load_m2l.wait()
    for part in range(4):
        came = ghosts.at[pl.ds(0, (32 if part else 31) * GHOST)]
        pltpu.make_async_remote_copy(
            src_ref=came, dst_ref=came, send_sem=send_sem, recv_sem=recv_sem.at[part],
            device_id=((g + 1) % 8, m), device_id_type=MESH,
        ).wait_recv()
        to_table(ghosts, part * 512, 512, tab, BOXES + part * 512)
        if part < 3:
            partial[...] += product(part + 1, ghosts[part * 512 : (part + 1) * 512, :])

    def pick_pair(stage, part):
        for u in range(2):
            for s in range(256):
                column = part * 16 + u * 8 + s // SLOTS
                pick(tab, (start_a, start_b)[stage][s % SLOTS, column], picks[2 * (part % 2) + u], s)

    def sum_pair(block, part):
        both = []
        for u in range(2):
            hot = one_hot(type_key[pl.ds(block * 16 + part * 2 + u, 1), :], TYPES * 8)
            rows = jnp.concatenate(picked_rows(picks[2 * (part % 2) + u], 256), axis=1)
            both.append(dot(hot, rows).reshape(TYPES, 8, WIDTH))
        row = pl.multiple_of(block * 128 + part * 16, 16)
        typed[:, pl.ds(row, 16), :] = jnp.concatenate(both, axis=1).astype(BF16)

    def leaf(block, carry):
        kinds = pl.ds((block - 1) * 4, 4)
        late = dot(counts[4, kinds].reshape(4 * 128, 2 * LO), ghosts[3 * 512 : 4 * 512, :])
        typed[kinds, 0:128, :] = (partial[kinds] + late.reshape(4, 128, WIDTH)).astype(BF16)
        for part in range(8):
            stage = part // 4
            if part % 4 == 0:
                fetch(block, stage).wait()
            pick_pair(stage, part)
            if part % 4 == 3:
                fetch(block + 1, stage).start()
            if part:
                sum_pair(block, part - 1)
        sum_pair(block, 7)
        return carry

    lax.fori_loop(1, 4, leaf, 0)
    fetch(0, 0).wait()
    fetch(0, 1).wait()

    total = out_ref[...]
    for t in range(TYPES):
        total = total + dot(typed[t], m2l[t])
    out_ref[...] = total

    went = outgoing.at[pl.ds(0, (DEVICES - 1) * GHOST)]
    pltpu.make_async_remote_copy(
        src_ref=went, dst_ref=went, send_sem=send_sem, recv_sem=recv_sem.at[0],
        device_id=((g + 1) % 8, m), device_id_type=MESH,
    ).wait_send()
    pltpu.make_async_remote_copy(
        src_ref=rest, dst_ref=rest, send_sem=psend_sem, recv_sem=precv_sem, device_id=((g + 1) % 8, m), device_id_type=MESH
    ).wait_send()


def shards(density, send_list, v_src, v_type, coarse_src, coarse_type, m2l_ops, coarse_ops, m2m_ops, l2l_ops):
    dma = pltpu.SemaphoreType.DMA
    return pl.pallas_call(
        kernel,
        out_shape=jax.ShapeDtypeStruct((BOXES, WIDTH), F32),
        in_specs=[pl.BlockSpec(memory_space=pltpu.HBM)] * 10,
        out_specs=pl.BlockSpec(memory_space=pltpu.VMEM),
        scratch_shapes=[
            pltpu.VMEM((BOXES, WIDTH), BF16),
            pltpu.SMEM((1, DEVICES * GHOST), I32),
            pltpu.VMEM((SLOTS, BOXES), I32),
            pltpu.VMEM((SLOTS, BOXES), I32),
            pltpu.VMEM((SLOTS, PARENTS), I32),
            pltpu.VMEM((SLOTS, PARENTS), I32),
            pltpu.VMEM((TYPES, WIDTH, WIDTH), BF16),
            pltpu.VMEM((TYPES, WIDTH, WIDTH), BF16),
            pltpu.VMEM((8, WIDTH, WIDTH), BF16),
            pltpu.VMEM((DEVICES * GHOST, WIDTH), BF16),
            pltpu.VMEM((DEVICES * GHOST, WIDTH), BF16),
            pltpu.VMEM((PARENTS, WIDTH), BF16),
            pltpu.VMEM((8 * PARENTS, WIDTH), BF16),
            pltpu.VMEM((TYPES, BOXES, WIDTH), BF16),
            pltpu.VMEM((PARENTS, 8, WIDTH), F32),
            pltpu.VMEM(((ROWS + 2) * CHUNKS, 128), F32),
            pltpu.VMEM((256 * CHUNKS, 128), F32),
            pltpu.VMEM((256 * CHUNKS, 128), F32),
            pltpu.VMEM((256 * CHUNKS, 128), F32),
            pltpu.VMEM((256 * CHUNKS, 128), F32),
            pltpu.SMEM((SLOTS, 128), I32),
            pltpu.SMEM((SLOTS, 128), I32),
            pltpu.VMEM((SLOTS, BOXES), I32),
            pltpu.VMEM((BOXES // 8, 8 * SLOTS), F32),
            pltpu.VMEM((1, PARENTS // 8, 8 * SLOTS), F32),
            pltpu.VMEM((PARENTS // 8, 8 * SLOTS), F32),
            pltpu.VMEM((1, TYPES, PARENTS, 2 * LO), BF16),
            pltpu.VMEM((5, 16, 8 * SLOTS), F32),
            pltpu.VMEM((16, 8 * SLOTS), F32),
            pltpu.VMEM((5, TYPES, 128, 2 * LO), BF16),
            pltpu.VMEM((TYPES, 128, WIDTH), F32),
            dma((6,)),
            dma((4,)),
            dma((2,)),
            dma,
            dma((4,)),
            dma,
            dma,
        ],
        compiler_params=pltpu.CompilerParams(
            collective_id=0, has_side_effects=True, vmem_limit_bytes=60 * 1024 * 1024
        ),
        cost_estimate=pl.CostEstimate(flops=8_000_000_000, bytes_accessed=30_000_000, transcendentals=0),
        name="far_field",
    )(density, send_list, v_src.T, v_type.T, coarse_src.T, coarse_type.T, m2l_ops, coarse_ops, m2m_ops, l2l_ops)


def solution(mesh):
    row = P(("morton", "grp"), None)
    return jax.shard_map(
        shards,
        mesh=mesh,
        in_specs=(row, row, row, row, row, row, P(), P(), P(), P()),
        out_specs=row,
        check_vma=False,
    )
```

```python
import jax
import jax.numpy as jnp
from jax import lax
from jax.experimental import pallas as pl
from jax.experimental.pallas import tpu as pltpu
from jax.sharding import PartitionSpec as P

MESH = pl.DeviceIdType.MESH
BF16 = jnp.bfloat16
F32 = jnp.float32
I32 = jnp.int32

DEVICES = 128
GHOST = 16
BOXES = 512
WIDTH = 512
TYPES = 12
SLOTS = 32
PARENTS = 64
LO = 256
KEYS = 2 * TYPES * 8
NONE = 255.0
ROWS = BOXES + DEVICES * GHOST
CHUNKS = WIDTH // 128


def dot(a, b):
    return jnp.dot(a, b, preferred_element_type=F32)


def dot_t(a, b):
    return lax.dot_general(a, b, (((1,), (1,)), ((), ())), preferred_element_type=F32)


def iota(shape, dim):
    return lax.broadcasted_iota(I32, shape, dim)


def to_lanes(values):
    n = values.shape[0]
    spread = (iota((SLOTS, 8 * SLOTS), 1) % SLOTS == iota((SLOTS, 8 * SLOTS), 0)).astype(F32).astype(BF16)
    wide = dot(values.astype(F32).astype(BF16), spread)
    own = iota((n, 8 * SLOTS), 0) % 8 == iota((n, 8 * SLOTS), 1) // SLOTS
    wide = jnp.where(own, wide, 0.0).astype(BF16)
    rows = (iota((n // 8, n), 1) // 8 == iota((n // 8, n), 0)).astype(F32).astype(BF16)
    return dot(rows, wide)


def write_keys(column, kind, parts, key_ref, lo_ref):
    n = column.shape[0]
    hi = column // LO
    key = to_lanes((hi % 2) * (TYPES * 8) + kind * 8 + iota((n, SLOTS), 0) % 8)
    part_row = to_lanes(hi // 2)
    lo_ref[...] = to_lanes(column % LO)
    for part in range(parts):
        key_ref[part] = jnp.where(part_row == float(part), key, NONE)


def one_hot(row, count):
    wide = jnp.broadcast_to(row, (16, row.shape[1])).astype(BF16)
    shape = (count // 16, 16, row.shape[1])
    index = (iota(shape, 0) * 16 + iota(shape, 1)).astype(F32).astype(BF16)
    return jnp.where(wide[None] == index, jnp.ones((), BF16), jnp.zeros((), BF16)).reshape(count, row.shape[1])


def build_counts(pair, parts, key_ref, lo_ref, count_ref):
    results = []
    for u in range(2):
        group = 2 * pair + u
        low = one_hot(lo_ref[pl.ds(group, 1), :], LO)
        hot = jnp.concatenate([one_hot(key_ref[part, pl.ds(group, 1), :], KEYS) for part in range(parts)], axis=0)
        results.append(dot_t(hot, low))
    row = pl.multiple_of(pair * 16, 16)
    for part in range(parts):
        for half in range(2):
            first = part * KEYS + half * (KEYS // 2)
            both = [r[first : first + KEYS // 2].reshape(TYPES, 8, LO) for r in results]
            count_ref[part, :, pl.ds(row, 16), half * LO : (half + 1) * LO] = jnp.concatenate(both, axis=1).astype(BF16)


def to_table(rows_ref, first, count, tab, at):
    for j in range(CHUNKS):
        part = rows_ref[first : first + count, j * 128 : (j + 1) * 128].astype(F32)
        tab[pl.ds(at * CHUNKS + j, count, stride=CHUNKS), :] = part


def pick(tab, start, picked, slot):
    picked[slot * CHUNKS : (slot + 1) * CHUNKS, :] = tab[pl.ds(start, CHUNKS), :]


def picked_rows(picked, count):
    return [picked[pl.ds(j, count, stride=CHUNKS), :].astype(BF16) for j in range(CHUNKS)]


def step_of(i):
    s = i // 32
    dy = (i // 8) % 4
    dz = (i // 2) % 4
    dc = i % 2
    dx = (s + 8 - dy - dz) % 4
    return dy, dc, dz, dx


def kernel(
    density_h, send_h, v_src_h, v_type_h, c_src_h, c_type_h, m2l_h, cops_h, m2m_h, l2l_h,
    out_ref,
    dens, send, v_src, v_type, c_src, c_type, m2l, cops, octant,
    outgoing, ghosts, parents, group, typed, from_parent, tab, pick_0, pick_1, pick_2, pick_3, start_a, start_b, scaled,
    type_key, ckey_ref, clo_ref, ccounts, key_ref, lo_ref, counts, partial,
    load_sem, weight_sem, index_sem, send_sem, recv_sem, psend_sem, precv_sem,
):
    g = lax.axis_index("grp")
    m = lax.axis_index("morton")
    me = g * 16 + m
    picks = (pick_0, pick_1, pick_2, pick_3)
    my, mc, mz, mx = g // 2, g % 2, m // 4, m % 4

    loads = []
    for j, (src, dst) in enumerate(
        ((density_h, dens), (send_h, send), (v_src_h, v_src), (v_type_h, v_type), (c_src_h, c_src), (c_type_h, c_type))
    ):
        loads.append(pltpu.make_async_copy(src, dst, load_sem.at[j]))
    load_m2m = pltpu.make_async_copy(m2m_h, octant, weight_sem.at[0])
    load_cops = pltpu.make_async_copy(cops_h, cops, weight_sem.at[1])
    load_m2l = pltpu.make_async_copy(m2l_h, m2l, weight_sem.at[2])
    load_l2l = pltpu.make_async_copy(l2l_h, octant, weight_sem.at[3])
    for load in loads[:2]:
        load.start()
    load_m2m.start()
    for load in loads[2:]:
        load.start()

    barrier = pltpu.get_barrier_semaphore()

    def greet(i, carry):
        other = (me + i) % DEVICES
        pl.semaphore_signal(barrier, inc=1, device_id=(other // 16, other % 16), device_id_type=MESH)
        return carry

    lax.fori_loop(1, DEVICES, greet, 0)

    loads[0].wait()
    to_table(dens, 0, BOXES, tab, 0)
    tab[ROWS * CHUNKS : (ROWS + 2) * CHUNKS, :] = jnp.zeros((2 * CHUNKS, 128), F32)
    loads[1].wait()

    for q in range(8):
        picked = picks[q % 4]
        for s in range(256):
            pick(tab, send[0, q * 256 + s] * CHUNKS, picked, s)
        for j, part in enumerate(picked_rows(picked, 256)):
            outgoing[q * 256 : (q + 1) * 256, j * 128 : (j + 1) * 128] = part

    ghosts[0:GHOST, :] = outgoing[pl.ds(pl.multiple_of(me * GHOST, GHOST), GHOST), :]

    pl.semaphore_wait(barrier, DEVICES - 1)

    def send_rows(i, carry):
        dy, dc, dz, dx = step_of(i)
        g2 = ((my + dy) % 4) * 2 + (mc + dc) % 2
        m2 = ((mz + dz) % 4) * 4 + (mx + dx) % 4
        there = pl.multiple_of((g2 * 16 + m2) * GHOST, GHOST)
        pltpu.make_async_remote_copy(
            src_ref=outgoing.at[pl.ds(there, GHOST)],
            dst_ref=ghosts.at[pl.ds(pl.multiple_of(i * GHOST, GHOST), GHOST)],
            send_sem=send_sem, recv_sem=recv_sem.at[i // 32],
            device_id=(g2, m2), device_id_type=MESH,
        ).start()
        return carry

    lax.fori_loop(1, 64, send_rows, 0)

    r = iota((BOXES, BOXES), 0)
    order = (iota((BOXES, BOXES), 1) == (r % PARENTS) * 8 + r // PARENTS).astype(F32).astype(BF16)
    by_octant = dot(order, dens[...]).astype(BF16)
    load_m2m.wait()
    total = dot(by_octant[0:PARENTS], octant[0])
    for k in range(1, 8):
        total = total + dot(by_octant[k * PARENTS : (k + 1) * PARENTS], octant[k])
    mine = total.astype(BF16)
    parents[...] = mine
    my_rows = pl.ds(pl.multiple_of(g * PARENTS, PARENTS), PARENTS)
    group[my_rows, :] = mine
    for i in range(1, 8):
        pltpu.make_async_remote_copy(
            src_ref=parents, dst_ref=group.at[my_rows], send_sem=psend_sem, recv_sem=precv_sem,
            device_id=((g + i) % 8, m), device_id_type=MESH,
        ).start()
    load_l2l.start()
    load_cops.start()
    load_m2l.start()
    lax.fori_loop(64, DEVICES, send_rows, 0)

    for load in loads[2:]:
        load.wait()
    source = v_src[...]
    beyond = jnp.maximum(source - BOXES, 0)
    sender = beyond // GHOST
    dx = (mx + 4 - sender % 4) % 4
    dz = (mz + 4 - (sender // 4) % 4) % 4
    dc = (mc + 2 - (sender // 16) % 2) % 2
    dy = (my + 4 - (sender // 32) % 4) % 4
    place = ((dx + dy + dz) % 4) * 32 + dy * 8 + dz * 2 + dc
    moved = BOXES + place * GHOST + beyond % GHOST
    column = jnp.where(source < BOXES, source, jnp.where(source < ROWS, moved, ROWS))
    scaled[...] = column * CHUNKS
    kinds = v_type[...].T
    type_key[...] = to_lanes(kinds * 8 + iota((BOXES, SLOTS), 0) % 8)
    write_keys(column[:, 0:128].T, kinds[0:128], 5, key_ref, lo_ref)
    write_keys(c_src[...].T, c_type[...].T, 1, ckey_ref, clo_ref)

    def build_leaf(pair, carry):
        build_counts(pair, 5, key_ref, lo_ref, counts)
        return carry

    lax.fori_loop(0, 8, build_leaf, 0)

    def product(part, rows):
        return dot(counts[part].reshape(TYPES * 128, 2 * LO), rows).reshape(TYPES, 128, WIDTH)

    partial[...] = product(0, dens[...])

    def build_coarse(pair, carry):
        build_counts(pair, 1, ckey_ref, clo_ref, ccounts)
        return carry

    lax.fori_loop(0, 4, build_coarse, 0)
    rest = group.at[pl.ds(0, 7 * PARENTS)]
    pltpu.make_async_remote_copy(
        src_ref=rest, dst_ref=rest, send_sem=psend_sem, recv_sem=precv_sem, device_id=((g + 1) % 8, m), device_id_type=MESH
    ).wait_recv()
    load_cops.wait()

    def coarse_step(t, total):
        summed = dot(ccounts[0, t], group[...]).astype(BF16)
        return total + dot(summed, cops[t])

    coarse = lax.fori_loop(0, TYPES, coarse_step, jnp.zeros((PARENTS, WIDTH), F32)).astype(BF16)
    load_l2l.wait()
    for k in range(8):
        from_parent[:, k, :] = dot(coarse, octant[k])
    out_ref[...] = from_parent[...].reshape(BOXES, WIDTH)

    def fetch(block, stage):
        first = pl.multiple_of(jnp.minimum(block, 3) * 128, 128)
        return pltpu.make_async_copy(scaled.at[:, pl.ds(first, 128)], (start_a, start_b)[stage], index_sem.at[stage])

    fetch(1, 0).start()
    fetch(1, 1).start()
    load_m2l.wait()
    for part in range(4):
        came = ghosts.at[pl.ds(0, (32 if part else 31) * GHOST)]
        pltpu.make_async_remote_copy(
            src_ref=came, dst_ref=came, send_sem=send_sem, recv_sem=recv_sem.at[part],
            device_id=((g + 1) % 8, m), device_id_type=MESH,
        ).wait_recv()
        to_table(ghosts, part * 512, 512, tab, BOXES + part * 512)
        if part < 3:
            partial[...] += product(part + 1, ghosts[part * 512 : (part + 1) * 512, :])

    def pick_pair(stage, part):
        for u in range(2):
            for s in range(256):
                column = part * 16 + u * 8 + s // SLOTS
                pick(tab, (start_a, start_b)[stage][s % SLOTS, column], picks[2 * (part % 2) + u], s)

    def sum_pair(block, part):
        both = []
        for u in range(2):
            hot = one_hot(type_key[pl.ds(block * 16 + part * 2 + u, 1), :], TYPES * 8)
            rows = jnp.concatenate(picked_rows(picks[2 * (part % 2) + u], 256), axis=1)
            both.append(dot(hot, rows).reshape(TYPES, 8, WIDTH))
        row = pl.multiple_of(block * 128 + part * 16, 16)
        typed[:, pl.ds(row, 16), :] = jnp.concatenate(both, axis=1).astype(BF16)

    def leaf(block, carry):
        kinds = pl.ds((block - 1) * 4, 4)
        late = dot(counts[4, kinds].reshape(4 * 128, 2 * LO), ghosts[3 * 512 : 4 * 512, :])
        typed[kinds, 0:128, :] = (partial[kinds] + late.reshape(4, 128, WIDTH)).astype(BF16)
        for part in range(8):
            stage = part // 4
            if part % 4 == 0:
                fetch(block, stage).wait()
            pick_pair(stage, part)
            if part % 4 == 3:
                fetch(block + 1, stage).start()
            if part:
                sum_pair(block, part - 1)
        sum_pair(block, 7)
        return carry

    lax.fori_loop(1, 4, leaf, 0)
    fetch(0, 0).wait()
    fetch(0, 1).wait()

    total = out_ref[...]
    for t in range(TYPES):
        total = total + dot(typed[t], m2l[t])
    out_ref[...] = total

    went = outgoing.at[pl.ds(0, (DEVICES - 1) * GHOST)]
    pltpu.make_async_remote_copy(
        src_ref=went, dst_ref=went, send_sem=send_sem, recv_sem=recv_sem.at[0],
        device_id=((g + 1) % 8, m), device_id_type=MESH,
    ).wait_send()
    pltpu.make_async_remote_copy(
        src_ref=rest, dst_ref=rest, send_sem=psend_sem, recv_sem=precv_sem, device_id=((g + 1) % 8, m), device_id_type=MESH
    ).wait_send()


def shards(density, send_list, v_src, v_type, coarse_src, coarse_type, m2l_ops, coarse_ops, m2m_ops, l2l_ops):
    dma = pltpu.SemaphoreType.DMA
    return pl.pallas_call(
        kernel,
        out_shape=jax.ShapeDtypeStruct((BOXES, WIDTH), F32),
        in_specs=[pl.BlockSpec(memory_space=pltpu.HBM)] * 10,
        out_specs=pl.BlockSpec(memory_space=pltpu.VMEM),
        scratch_shapes=[
            pltpu.VMEM((BOXES, WIDTH), BF16),
            pltpu.SMEM((1, DEVICES * GHOST), I32),
            pltpu.VMEM((SLOTS, BOXES), I32),
            pltpu.VMEM((SLOTS, BOXES), I32),
            pltpu.VMEM((SLOTS, PARENTS), I32),
            pltpu.VMEM((SLOTS, PARENTS), I32),
            pltpu.VMEM((TYPES, WIDTH, WIDTH), BF16),
            pltpu.VMEM((TYPES, WIDTH, WIDTH), BF16),
            pltpu.VMEM((8, WIDTH, WIDTH), BF16),
            pltpu.VMEM((DEVICES * GHOST, WIDTH), BF16),
            pltpu.VMEM((DEVICES * GHOST, WIDTH), BF16),
            pltpu.VMEM((PARENTS, WIDTH), BF16),
            pltpu.VMEM((8 * PARENTS, WIDTH), BF16),
            pltpu.VMEM((TYPES, BOXES, WIDTH), BF16),
            pltpu.VMEM((PARENTS, 8, WIDTH), F32),
            pltpu.VMEM(((ROWS + 2) * CHUNKS, 128), F32),
            pltpu.VMEM((256 * CHUNKS, 128), F32),
            pltpu.VMEM((256 * CHUNKS, 128), F32),
            pltpu.VMEM((256 * CHUNKS, 128), F32),
            pltpu.VMEM((256 * CHUNKS, 128), F32),
            pltpu.SMEM((SLOTS, 128), I32),
            pltpu.SMEM((SLOTS, 128), I32),
            pltpu.VMEM((SLOTS, BOXES), I32),
            pltpu.VMEM((BOXES // 8, 8 * SLOTS), F32),
            pltpu.VMEM((1, PARENTS // 8, 8 * SLOTS), F32),
            pltpu.VMEM((PARENTS // 8, 8 * SLOTS), F32),
            pltpu.VMEM((1, TYPES, PARENTS, 2 * LO), BF16),
            pltpu.VMEM((5, 16, 8 * SLOTS), F32),
            pltpu.VMEM((16, 8 * SLOTS), F32),
            pltpu.VMEM((5, TYPES, 128, 2 * LO), BF16),
            pltpu.VMEM((TYPES, 128, WIDTH), F32),
            dma((6,)),
            dma((4,)),
            dma((2,)),
            dma,
            dma((4,)),
            dma,
            dma,
        ],
        compiler_params=pltpu.CompilerParams(
            collective_id=0, has_side_effects=True, vmem_limit_bytes=60 * 1024 * 1024
        ),
        cost_estimate=pl.CostEstimate(flops=8_000_000_000, bytes_accessed=30_000_000, transcendentals=0),
        name="far_field",
    )(density, send_list, v_src.T, v_type.T, coarse_src.T, coarse_type.T, m2l_ops, coarse_ops, m2m_ops, l2l_ops)


def solution(mesh):
    row = P(("morton", "grp"), None)
    return jax.shard_map(
        shards,
        mesh=mesh,
        in_specs=(row, row, row, row, row, row, P(), P(), P(), P()),
        out_specs=row,
        check_vma=False,
    )
```
